256 devices in a mesh: seq: 16 (over x_hi, y, core), exp: 16 (over x_lo, z).
Axes of the slice: x: 4 (x_hi: 2, x_lo: 2; x = x_hi * 2 + x_lo), y: 4, z: 8, core: 2. Of those that a mesh axis runs over, the one named last changes fastest.
Arguments:
- residual: bfloat16 [2048, 5120], P('seq', 'exp'), may hold values from -16 to 16
- query_nope: bfloat16 [2048, 8192], P('seq', 'exp'), may hold values from -8 to 8
- query_rope: bfloat16 [2048, 4096], P('seq', 'exp'), may hold values from -400 to 400
- latent: bfloat16 [2048, 512], P('seq'), may hold values from -6 to 6
- key_rope: bfloat16 [2048, 64], P('seq'), may hold values from -4 to 4
- key_lift: bfloat16 [64, 512, 128], P('exp'), may hold values from -0.25 to 0.25
- value_lift: bfloat16 [64, 512, 128], P('exp'), may hold values from -0.5 to 0.5
- out_weight: bfloat16 [8192, 5120], P('exp'), may hold values from -0.375 to 0.375
- norm_gain: float32 [5120], P('exp'), may hold values from 0.5 to 1.5
- gate_up_weight: bfloat16 [32, 5120, 3072], P('seq', 'exp'), may hold values from -0.125 to 0.125
- down_weight: bfloat16 [32, 1536, 5120], P('seq', None, 'exp'), may hold values from -0.625 to 0.625
- route_ids: int32 [2048, 6], P('seq'), may hold values from 0 to 31, all different within a row; in each aligned block of 128 rows (0 to 127, 128 to 255, ...) at most 48 rows name the same one
- route_weights: float32 [2048, 6], P('seq'), may hold values from 0.05 to 0.5
Outputs:
- out: bfloat16 [2048, 5120], P('seq', 'exp')
The draws below stay inside these ranges and needn't reach their ends.
Inputs may be any that keep to these rules, and one draw needn't show every extreme that they name: `route_ids`: each row names 6 different experts. Within each aligned block of 128 rows (the tokens of one sequence shard) no expert is named by more than 48 rows, and in some blocks one expert is named by exactly 48 rows.
All inputs are finite; a program needn't handle non-finite values.
Results may differ from the reference program's by a relative error of at most 0.029.
Values may be sent and summed in bfloat16 or wider, within the bound.
No kernel may reach another device: no remote copies, remote signals or barrier semaphores. Data moves between devices by JAX's collectives and lax.ppermute only.
A program may use at most 128 MiB of HBM per device.

```python
import math
import jax
import jax.numpy as jnp
import numpy as np
from jax import lax

D = 5120
HEADS = 64
NOPE = 128
ROPE = 64
VDIM = 128
LAT = 512
FF = 1536
TOPK = 6
SEQ_DEV = 128
CAP = 48
LEN = 2048
EXPERTS = 32
N_SEQ = 16
N_EXP = 16


def aligned_pair(key, aligned_count, low_strength, high_strength):
    key_base, query_base, pick_key, strength_key = jax.random.split(key, 4)
    keys = jnp.clip(jax.random.normal(key_base, (LEN, ROPE), jnp.float32), -4.0, 4.0)
    queries = jnp.clip(jax.random.normal(query_base, (LEN, HEADS, ROPE), jnp.float32), -6.0, 6.0)
    places = jnp.arange(LEN, dtype=jnp.int32)
    picked = (jax.random.randint(pick_key, (LEN,), 0, 32) < aligned_count) & (places % 2 == 1)
    strength = jax.random.uniform(strength_key, (LEN,), jnp.float32, low_strength, high_strength)
    queries = jnp.where(picked[:, None, None], strength[:, None, None] * keys[:, None, :], queries)
    score_scale = 1.0 / math.sqrt(NOPE + ROPE)
    shrink = 1.0 - 2.0 / (score_scale * strength * ROPE)
    following = jnp.roll(picked, -1)
    keys = jnp.where(following[:, None], jnp.roll(keys * shrink[:, None], -1, axis=0), keys)
    return (keys, queries.reshape(LEN, HEADS * ROPE))


def draw_key_rope(key, part):
    keys, queries = aligned_pair(key, 0, 25.0, 90.0)
    return keys.astype(jnp.bfloat16)


def draw_query_rope(key, part):
    keys, queries = aligned_pair(key, 0, 25.0, 90.0)
    return queries.astype(jnp.bfloat16)


def draw_residual(key, part):
    key = jax.random.fold_in(key, 3)
    base_key, jitter_key, row_key = jax.random.split(key, 3)
    column = jnp.arange(D, dtype=jnp.float32) / D
    jitter = jax.random.uniform(jitter_key, (D,), jnp.float32)
    column_scale = jnp.exp(math.log(10.0) * (0.5 * column + 0.5 * jitter - 1.0))
    row_scale = jnp.exp(jax.random.uniform(row_key, (LEN, 1), jnp.float32, -1.15, 1.15))
    values = jax.random.normal(base_key, (LEN, D), jnp.float32) * row_scale * column_scale
    return jnp.clip(values, -16.0, 16.0).astype(jnp.bfloat16)


def with_spikes(entries, rng, source, target, parts, factor):
    def block_of(position):
        return (jnp.arange(entries.shape[position]) // (entries.shape[position] // parts)).reshape((-1,) + (1,) * (entries.ndim - 1 - position))

    one_side = jax.random.permutation(rng, parts)[block_of(target)]
    far = (block_of(target) + parts // 2) % parts
    return jnp.where((block_of(source) == one_side) | (block_of(source) == far), factor * entries, entries)


def steps_of(key, extent, cuts, smallest, top_value):
    def one(dim, shards_of):
        heights = jax.random.uniform(jax.random.fold_in(jax.random.fold_in(key, 6), dim), (shards_of,), jnp.float32, smallest / len(cuts), top_value / len(cuts))
        return jnp.repeat(jnp.exp(heights), extent[dim] // shards_of).reshape((-1,) + (1,) * (len(extent) - dim - 1))

    level = one(*cuts[0])
    for cut in cuts[1:]:
        level = level * one(*cut)
    return level


def deal_out(rng, own, number, rows, number_of, top, limit, skew):
    sequence = jax.random.permutation(rng, number_of)
    crowded, usual = load_shares(number_of, rows * top, limit, skew, True), load_shares(number_of, rows * top, limit, skew, False)
    places = jnp.arange(number_of)

    def named(tallies, turn):
        used = int((tallies > 0).sum())
        fixed = max(1, used // 4)
        shifted = fixed + (places - fixed + turn * (used - fixed)) % max(1, number_of - fixed)
        return jnp.zeros((number_of,), jnp.int32).at[sequence[jnp.where(places < fixed, places, shifted)]].set(jnp.asarray(tallies, jnp.int32))

    tallies = jnp.where(number % 4 == 0, named(crowded, number // 4), named(usual, number - number // 4 - 1))
    mixed = jax.random.permutation(jax.random.fold_in(own, 3), number_of)
    giver, taker = mixed[0:number_of // 2 * 2:2], mixed[1:number_of // 2 * 2:2]
    room = jnp.minimum(tallies[giver] - 1, limit - tallies[taker]) // 2
    room = jnp.where((giver == sequence[0]) | (taker == sequence[0]) | (tallies[taker] == 0), 0, jnp.maximum(room, 0))
    shifted = jax.random.randint(jax.random.fold_in(own, 4), (number_of // 2,), 0, 1 << 20) % (room + 1)
    tallies = tallies.at[giver].add(-shifted).at[taker].add(shifted)
    items = jnp.searchsorted(jnp.cumsum(tallies), jnp.arange(rows * top), side="right").astype(jnp.int32)
    grid = items.reshape(top, rows).T
    grid = grid[jax.random.permutation(jax.random.fold_in(own, 1), rows)]
    turn = jax.random.randint(jax.random.fold_in(own, 2), (rows, 1), 0, top)
    return jnp.take_along_axis(grid, (jnp.arange(top)[None, :] + turn) % top, axis=1)


def load_shares(number_of, total, most, slope, full):
    portions = [(1 << 20) // math.isqrt(rank ** slope) + 1 for rank in range(1, number_of + 1)]
    largest = most if full else min(most, max(-(-total // number_of), total * portions[0] // sum(portions)))
    least = 1 if total - largest >= number_of - 1 else 0
    holding, rest = [largest] + [least] * (number_of - 1), total - largest - least * (number_of - 1)
    while rest > 0:
        candidates = [i for i in range(1, number_of) if holding[i] < largest] or [i for i in range(1, number_of) if holding[i] < most]
        whole, budget = sum([portions[i] for i in candidates]), rest
        for i in candidates:
            more = min(most - holding[i], max(1, budget * portions[i] // whole), rest)
            holding[i] = holding[i] + more
            rest = rest - more
    return np.array(holding)


def bell_draw(rng, extent, deviation, reach, cuts=(), kind=jnp.bfloat16):
    array = deviation * jax.random.normal(rng, extent, jnp.float32)
    if cuts:
        array = array * steps_of(rng, extent, cuts, -0.22, 0.18)
    return jnp.clip(array, -reach, reach).astype(kind)


def noise_with(key, shape, width, most, cuts, heavy, kind=jnp.bfloat16):
    values = width * jax.random.normal(key, shape, jnp.float32)
    if cuts:
        values = values * steps_of(key, shape, cuts, -0.22, 0.18)
    return jnp.clip(with_spikes(values, jax.random.fold_in(key, 3), *heavy), -most, most).astype(kind)


def setup_inputs(seed: int = 0) -> dict:
    seeds = jax.random.split(jax.random.key(seed), 14)
    residual = draw_residual(jax.random.fold_in(seeds[13], 71), 0)
    query_nope = bell_draw(seeds[1], (LEN, HEADS * NOPE), 2.0, 8.0, ((0, 16), (1, 16)))
    query_rope = draw_query_rope(jax.random.fold_in(seeds[13], 71), 0)
    latent = bell_draw(seeds[3], (LEN, LAT), 1.0, 6.0, ((0, 16),))
    key_rope = draw_key_rope(jax.random.fold_in(seeds[13], 71), 0)
    key_lift = bell_draw(seeds[5], (HEADS, LAT, NOPE), LAT ** -0.5, 0.25, ((0, 16),))
    value_lift = bell_draw(seeds[6], (HEADS, LAT, VDIM), (LAT // 4) ** -0.5, 0.5, ((0, 16),))
    out_weight = noise_with(seeds[7], (HEADS * VDIM, D), (HEADS * VDIM // 16) ** -0.5, 0.375, ((0, 16),), (0, 1, 16, 2.0))
    norm_gain = jnp.clip(1.0 + 0.1 * jax.random.normal(seeds[8], (D,), jnp.float32), 0.5, 1.5)
    gate_up_weight = noise_with(seeds[9], (EXPERTS, D, 2 * FF), D ** -0.5, 0.125, ((0, 16), (1, 16)), (1, 2, 16, 2.0))
    down_weight = bell_draw(seeds[10], (EXPERTS, FF, D), (FF // 16) ** -0.5, 0.625, ((0, 16), (2, 16)))
    route_ids_keys = jax.random.split(jax.random.fold_in(seeds[11], 1), LEN // SEQ_DEV)
    route_ids_turns = jax.random.permutation(jax.random.fold_in(seeds[11], 3), LEN // SEQ_DEV)
    route_ids = jax.vmap(lambda own, number: deal_out(jax.random.fold_in(seeds[11], 2), own, number, SEQ_DEV, EXPERTS, TOPK, CAP, 2))(route_ids_keys, route_ids_turns).reshape((LEN, TOPK))
    route_weights = jnp.clip(jnp.exp(math.log(0.5) - 2.3025851 * jax.random.uniform(seeds[12], (LEN, TOPK), jnp.float32) ** steps_of(seeds[12], (LEN, TOPK), ((0, 16),), -0.2, 0.2)), 0.05, 0.5)
    return {"residual": residual, "query_nope": query_nope, "query_rope": query_rope, "latent": latent, "key_rope": key_rope, "key_lift": key_lift, "value_lift": value_lift, "out_weight": out_weight, "norm_gain": norm_gain, "gate_up_weight": gate_up_weight, "down_weight": down_weight, "route_ids": route_ids, "route_weights": route_weights}


def reference(residual, query_nope, query_rope, latent, key_rope, key_lift, value_lift, out_weight, norm_gain, gate_up_weight, down_weight, route_ids, route_weights):
    score_scale = 1.0 / (NOPE + ROPE) ** 0.5
    query_heads = query_nope.reshape(LEN, HEADS, NOPE).astype(jnp.float32)
    query_latent = jnp.einsum('thn,hln->htl', query_heads, key_lift.astype(jnp.float32)).astype(jnp.bfloat16)
    query_rotary = jnp.transpose(query_rope.reshape(LEN, HEADS, ROPE), (1, 0, 2))
    places = jnp.arange(LEN, dtype=jnp.int32)
    allowed = places[None, :] <= places[:, None]

    def head_output(operands):
        head_latent, head_rotary, head_lift = operands
        scores = jnp.dot(head_latent, latent.T, preferred_element_type=jnp.float32)
        scores = (scores + jnp.dot(head_rotary, key_rope.T, preferred_element_type=jnp.float32)) * score_scale
        highest = lax.optimization_barrier(jnp.max(jnp.where(allowed, scores, -jnp.inf), axis=1, keepdims=True))
        weights = jnp.where(allowed, jnp.exp(scores - highest), 0.0)
        total_mass = lax.optimization_barrier(jnp.sum(weights, axis=1, keepdims=True))
        merged = jnp.dot(weights.astype(jnp.bfloat16), latent, preferred_element_type=jnp.float32)
        attended = (merged / total_mass).astype(jnp.bfloat16)
        return jnp.dot(attended, head_lift, preferred_element_type=jnp.float32).astype(jnp.bfloat16)
    head_values = lax.map(head_output, (query_latent, query_rotary, value_lift))
    flat_values = jnp.transpose(head_values, (1, 0, 2)).reshape(LEN, HEADS * VDIM)
    attention = jnp.dot(flat_values, out_weight, preferred_element_type=jnp.float32)
    mixed = (residual.astype(jnp.float32) + attention).astype(jnp.bfloat16)
    mixed_float = mixed.astype(jnp.float32)
    mean_square = lax.optimization_barrier(jnp.mean(mixed_float * mixed_float, axis=1, keepdims=True))
    normed = (mixed_float * lax.rsqrt(mean_square + 1e-06) * norm_gain).astype(jnp.bfloat16)
    block_rows = SEQ_DEV * TOPK
    blocks = route_ids.reshape(N_SEQ, block_rows)
    onehot = (blocks[:, :, None] == jnp.arange(EXPERTS, dtype=jnp.int32)[None, None, :]).astype(jnp.int32)
    earlier = jnp.cumsum(onehot, axis=1).astype(jnp.int32) - onehot
    row_ranks = lax.optimization_barrier(jnp.sum(earlier * onehot, axis=2)).astype(jnp.int32)
    row_slots = blocks * CAP + row_ranks
    block_tokens = jnp.arange(N_SEQ, dtype=jnp.int32)[:, None] * SEQ_DEV + jnp.arange(block_rows, dtype=jnp.int32)[None, :] // TOPK
    matches = row_slots[:, :, None] == jnp.arange(EXPERTS * CAP, dtype=jnp.int32)[None, None, :]
    slot_tokens = (lax.optimization_barrier(jnp.sum(jnp.where(matches, block_tokens[:, :, None] + 1, 0), axis=1)) - 1).astype(jnp.int32)
    slot_order = jnp.transpose(slot_tokens.reshape(N_SEQ, EXPERTS, CAP), (1, 0, 2)).reshape(EXPERTS, N_SEQ * CAP)

    def expert_output(operands):
        token_index, expert_gate_up, expert_down = operands
        token_rows = jnp.take(normed, jnp.maximum(token_index, 0), axis=0)
        token_rows = jnp.where((token_index >= 0)[:, None], token_rows, jnp.zeros_like(token_rows))
        grouped = token_rows.reshape(N_SEQ * CAP, N_EXP, D // N_EXP).astype(jnp.float32)
        lifted = expert_gate_up.reshape(N_EXP, D // N_EXP, 2 * FF).astype(jnp.float32)
        partial_value = jnp.einsum('rgc,gcf->grf', grouped, lifted).astype(jnp.bfloat16)
        partial_value = lax.optimization_barrier(partial_value)
        summed = lax.optimization_barrier(jnp.sum(partial_value.astype(jnp.float32), axis=0))
        activated = (jax.nn.silu(summed[:, :FF]) * summed[:, FF:]).astype(jnp.bfloat16)
        return jnp.dot(activated, expert_down, preferred_element_type=jnp.float32).astype(jnp.bfloat16)
    expert_rows = lax.map(expert_output, (slot_order, gate_up_weight, down_weight))
    block_index = (jnp.arange(LEN, dtype=jnp.int32) // SEQ_DEV)[:, None]
    slot_places = (block_index * CAP + row_ranks.reshape(LEN, TOPK)).astype(jnp.int32)
    picked = expert_rows[route_ids, slot_places].astype(jnp.float32)
    routed = lax.optimization_barrier(jnp.sum(picked * route_weights[:, :, None], axis=1))
    return (mixed_float + routed).astype(jnp.bfloat16)
```

```python
import functools
import math

import jax
import jax.numpy as jnp
from jax import lax
from jax.experimental import pallas as pl
from jax.experimental.pallas import tpu as pltpu
from jax.sharding import Mesh, PartitionSpec as P

CAP = 48
NORM_EPS = 1e-06
BF = jnp.bfloat16
F32 = jnp.float32

AXES = ("xh", "y", "core", "xl", "z")
SEQ = ("xh", "y", "core")
EXP = ("xl", "z")
NX, NY, NZ = 4, 4, 8


def xor_x(value, bits):
    return lax.ppermute(value, ("xh", "xl"), [(s, s ^ bits) for s in range(NX)])


def from_y(value, ahead):
    return lax.ppermute(value, "y", [(s, (s - ahead) % NY) for s in range(NY)])


def swap_core(value):
    return lax.ppermute(value, "core", [(0, 1), (1, 0)])


def to_z(value, ahead):
    return lax.ppermute(value, "z", [(s, (s + ahead) % NZ) for s in range(NZ)])


def to_owner(value, step):
    pairs = []
    for xh in range(2):
        for y in range(NY):
            for z in range(NZ):
                chunk = (z + step) % NZ
                xh_to, y_to = xh ^ (chunk // NY), (y + chunk % NY) % NY
                pairs.append(((xh * NY + y) * NZ + z, (xh_to * NY + y_to) * NZ + z))
    return lax.ppermute(value, ("xh", "y", "z"), pairs)


def vmem_call(kernel, out_shape, in_specs, scratch, flops, name):
    outs = jax.tree.map(lambda _: pl.BlockSpec(memory_space=pltpu.VMEM), out_shape)
    return pl.pallas_call(
        kernel,
        out_shape=out_shape,
        in_specs=in_specs,
        out_specs=outs,
        scratch_shapes=scratch,
        compiler_params=pltpu.CompilerParams(vmem_limit_bytes=48 * 2**20),
        cost_estimate=pl.CostEstimate(flops=flops, bytes_accessed=8 * 2**20, transcendentals=0),
        name=name,
    )


VMEM = pl.BlockSpec(memory_space=pltpu.VMEM)
SMEM = pl.BlockSpec(memory_space=pltpu.SMEM)
HBM = pl.BlockSpec(memory_space=pl.ANY)


def attention_kernel(score_scale, pieces, base_ref, q_ref, *refs):
    kv_refs = refs[:pieces]
    places_ref, lift_ref, weight_ref, out_ref, scores_ref, values_ref = refs[pieces:]
    heads, rows, _ = q_ref.shape
    keys = kv_refs[0].shape[0]
    width = lift_ref.shape[1]
    query_places = base_ref[0] + lax.broadcasted_iota(jnp.int32, (rows, keys), 0)
    for h in range(heads):
        for p in range(pieces):
            scores = lax.dot_general(
                q_ref[h], kv_refs[p][...], (((1,), (1,)), ((), ())), preferred_element_type=F32
            )
            allowed = places_ref[:, p * keys : (p + 1) * keys] <= query_places
            scores_ref[:, p * keys : (p + 1) * keys] = jnp.where(
                allowed, scores * score_scale, -1e30
            )
        top = jnp.max(scores_ref[...], axis=1, keepdims=True)
        mass = jnp.zeros((rows, 1), F32)
        total = jnp.zeros((rows, width), F32)
        for p in range(pieces):
            weights = jnp.exp(scores_ref[:, p * keys : (p + 1) * keys] - top)
            mass = mass + jnp.sum(weights, axis=1, keepdims=True)
            total = total + jnp.dot(
                weights.astype(BF), kv_refs[p][:, :width], preferred_element_type=F32
            )
        attended = (total / mass).astype(BF)
        value_width = lift_ref.shape[2]
        values_ref[:, h * value_width : (h + 1) * value_width] = jnp.dot(
            attended, lift_ref[h], preferred_element_type=F32
        ).astype(BF)
    for c in range(out_ref.shape[0]):
        out_ref[c] = jnp.dot(
            values_ref[...], weight_ref[c], preferred_element_type=F32
        ).astype(BF)


def slot_matrix(places, rows):
    ranks = lax.broadcasted_iota(jnp.int32, (rows, places.shape[1]), 0)
    return jnp.where(ranks == places, 1.0, 0.0)


def gate_up_kernel(z_ref, *refs):
    token_refs = refs[:8]
    place_ref, weight_ref, out_ref, tokens_ref, rows_ref, sems = refs[8:]
    tokens = token_refs[0].shape[1]
    copies = []
    for piece in range(8):
        ahead, core = piece // 2, piece % 2
        for jx in range(2):
            copies.append(
                pltpu.make_async_copy(
                    token_refs[piece].at[jx],
                    tokens_ref.at[jx * NY + ahead, pl.ds(core * tokens, tokens)],
                    sems.at[piece * 2 + jx],
                )
            )
    for copy in copies:
        copy.start()
    for copy in copies:
        copy.wait()
    for k in range(NZ):
        chunk = (z_ref[0] + k) % NZ
        places = place_ref[chunk]
        empty = jnp.zeros((CAP, tokens), F32)
        parts = []
        for e in range(2):
            for c in range(2):
                own = slot_matrix(places[e * 2 + c : e * 2 + c + 1], CAP)
                parts.append(jnp.concatenate([own, empty] if c == 0 else [empty, own], axis=1))
        picks = jnp.concatenate(parts, axis=0).astype(BF)
        rows = jnp.dot(picks, tokens_ref[chunk], preferred_element_type=F32).astype(BF)
        for e in range(2):
            rows_ref[e, k] = rows[e * 2 * CAP : (e + 1) * 2 * CAP]
    width = weight_ref.shape[1]
    for e in range(2):
        for k in range(0, NZ, 2):
            rows = rows_ref[e, k : k + 2].reshape(4 * CAP, width)
            hidden = jnp.dot(rows, weight_ref[e], preferred_element_type=F32).astype(BF)
            out_ref[k, e] = hidden[: 2 * CAP]
            out_ref[k + 1, e] = hidden[2 * CAP :]


def down_kernel(act0_ref, act1_ref, weight_ref, place_ref, gain_ref, own_ref, other_ref):
    outs = [
        jnp.dot(act[...], weight_ref[e], preferred_element_type=F32)
        for e, act in enumerate((act0_ref, act1_ref))
    ]
    for c, out_ref in enumerate((own_ref, other_ref)):
        picks, rows = [], []
        for e in range(2):
            pick = slot_matrix(place_ref[e * 2 + c : e * 2 + c + 1], CAP)
            gain = jnp.sum(pick * gain_ref[e * 2 + c : e * 2 + c + 1], axis=1, keepdims=True)
            picks.append(pick)
            rows.append(outs[e][c * CAP : (c + 1) * CAP] * gain)
        out_ref[...] = lax.dot_general(
            jnp.concatenate(picks, axis=0).astype(BF),
            jnp.concatenate(rows, axis=0).astype(BF),
            (((0,), (0,)), ((), ())),
            preferred_element_type=F32,
        ).astype(BF)


def body(
    residual,
    query_nope,
    query_rope,
    latent,
    key_rope,
    key_lift,
    value_lift,
    out_weight,
    norm_gain,
    gate_up_weight,
    down_weight,
    route_ids,
    route_weights,
):
    rows, columns = residual.shape
    heads, width, nope = key_lift.shape
    rope = key_rope.shape[1]
    topk = route_ids.shape[1]
    hidden = down_weight.shape[1]
    half_hidden = hidden // 2
    half_rows = rows // 2
    model_width = out_weight.shape[1]
    score_scale = 1.0 / math.sqrt(nope + rope)
    xh, y, core = lax.axis_index("xh"), lax.axis_index("y"), lax.axis_index("core")
    xl, z = lax.axis_index("xl"), lax.axis_index("z")
    shard = (xh * NY + y) * 2 + core

    with jax.named_scope("gather_keys"):
        weight_high = route_weights.astype(BF)
        rest = route_weights - weight_high.astype(F32)
        weight_mid = rest.astype(BF)
        weight_low = (rest - weight_mid.astype(F32)).astype(BF)
        packed_width = 640
        filler = packed_width - width - rope - 4 * topk
        packed = jnp.concatenate(
            [
                latent,
                key_rope,
                route_ids.astype(BF),
                weight_high,
                weight_mid,
                weight_low,
                jnp.zeros((rows, filler), BF),
            ],
            axis=1,
        )
        packed = lax.dynamic_slice_in_dim(packed, xl * half_rows, half_rows, axis=0)
        along_x = jnp.concatenate([packed] + [xor_x(packed, bits) for bits in (1, 2, 3)], axis=0)
        pieces = []
        for ahead in range(NY):
            mine = along_x if ahead == 0 else from_y(along_x, ahead)
            pieces += [mine, swap_core(mine)]

    with jax.named_scope("swap_weights"):
        split = gate_up_weight.reshape(2, columns, 2, 2, half_hidden)
        keep = lax.dynamic_index_in_dim(split, xl, axis=3, keepdims=False)
        give = lax.dynamic_index_in_dim(split, 1 - xl, axis=3, keepdims=False)
        keep = keep.reshape(2, columns, hidden)
        taken = xor_x(give.reshape(2, columns, hidden), 1)
        up_weight = jnp.concatenate([keep, taken], axis=1)
        split = down_weight.reshape(2, 2, half_hidden, columns)
        keep = lax.dynamic_index_in_dim(split, xl, axis=1, keepdims=False)
        give = lax.dynamic_index_in_dim(split, 1 - xl, axis=1, keepdims=False)
        low_weight = jnp.concatenate([keep, xor_x(give, 1)], axis=2)

    with jax.named_scope("attention"):
        query_heads = query_nope.reshape(rows, heads, nope)
        query_latent = jnp.einsum(
            "thn,hln->htl", query_heads, key_lift, preferred_element_type=F32
        ).astype(BF)
        query_rotary = jnp.transpose(query_rope.reshape(rows, heads, rope), (1, 0, 2))
        queries = jnp.concatenate(
            [query_latent, query_rotary, jnp.zeros((heads, rows, rope), BF)], axis=2
        )
        split = out_weight.reshape(heads * value_lift.shape[2], 2, NZ, columns)
        mine = lax.dynamic_index_in_dim(split, xl, axis=1, keepdims=False)
        other = lax.dynamic_index_in_dim(split, 1 - xl, axis=1, keepdims=False)
        mix_weight = jnp.transpose(jnp.concatenate([mine, other], axis=2), (1, 0, 2))
        starts = []
        for ahead in range(NY):
            for flip in range(2):
                for bits in range(NX):
                    block = ((xh ^ (bits // 2)) * NY + (y + ahead) % NY) * 2 + (core ^ flip)
                    starts.append(block * rows + (xl ^ (bits % 2)) * half_rows)
        places = (
            jnp.stack(starts)[:, None] + jnp.arange(half_rows, dtype=jnp.int32)[None, :]
        ).reshape(1, -1)
        partial_mix = vmem_call(
            functools.partial(attention_kernel, score_scale, len(pieces)),
            jax.ShapeDtypeStruct((NZ, rows, 2 * columns), BF),
            [SMEM] + [VMEM] * (len(pieces) + 4),
            [
                pltpu.VMEM((rows, places.shape[1]), F32),
                pltpu.VMEM((rows, heads * value_lift.shape[2]), BF),
            ],
            4 * 10**9,
            "attention",
        )((shard * rows).reshape(1), queries, *pieces, places, value_lift, mix_weight)

    with jax.named_scope("routing"):
        notes = [piece[:, width + rope : width + rope + 4 * topk] for piece in pieces]
        notes = jnp.stack(notes).reshape(NY, 2, 2, 2, half_rows, 4 * topk)
        notes = jnp.where(xl == 0, notes, notes[:, :, :, ::-1])
        notes = jnp.transpose(notes.reshape(NY, 2, 2, rows, 4 * topk), (4, 2, 0, 1, 3)).astype(F32)
        ids, gains = notes[:topk], notes[topk : 2 * topk]
        gains = gains + notes[2 * topk : 3 * topk] + notes[3 * topk :]
        masks, weights = [], []
        for e in range(2):
            named = ids == (2 * shard + e).astype(F32)
            masks.append(jnp.max(jnp.where(named, 1.0, 0.0), axis=0))
            weights.append(jnp.sum(jnp.where(named, gains, 0.0), axis=0))
        mask = jnp.stack(masks, axis=2)
        gain = jnp.stack(weights, axis=2).reshape(NZ, 4, rows)
        earlier = jnp.triu(jnp.ones((rows, rows), BF), 1)
        rank = jnp.dot(mask.reshape(-1, rows).astype(BF), earlier, preferred_element_type=F32)
        place = jnp.where(mask.reshape(-1, rows) > 0, rank, -1.0).astype(jnp.int32)
        place = place.reshape(NZ, 4, rows)

    with jax.named_scope("sum_mix"):

        def own(step):
            return lax.dynamic_index_in_dim(partial_mix, (z + step) % NZ, 0, keepdims=False)

        def plus(a, b):
            return (a.astype(F32) + b.astype(F32)).astype(BF)

        top, low = own(4)[:half_rows], own(4)[half_rows:]
        ahead_in = to_z(top, 1)
        back_in = to_z(low, -1)
        for step in (3, 2, 1):
            ahead_out, back_out = own(step), own(-step)
            if step == 3:
                ahead_out = jnp.concatenate(
                    [plus(ahead_out[:half_rows], ahead_in), ahead_out[half_rows:]], axis=0
                )
                back_out = jnp.concatenate(
                    [back_out[:half_rows], plus(back_out[half_rows:], back_in)], axis=0
                )
            else:
                ahead_out, back_out = plus(ahead_out, ahead_in), plus(back_out, back_in)
            ahead_in, back_in = to_z(ahead_out, 1), to_z(back_out, -1)
        mix = own(0).astype(F32) + ahead_in.astype(F32) + back_in.astype(F32)
        mix = mix[:, :columns] + xor_x(mix[:, columns:].astype(BF), 1).astype(F32)

    with jax.named_scope("norm"):
        mixed = (residual.astype(F32) + mix).astype(BF)
        mixed_float = mixed.astype(F32)
        squares = jnp.sum(mixed_float * mixed_float, axis=1)
        squares = squares + xor_x(squares, 1)
        total = squares
        for ahead in range(1, NZ):
            total = total + to_z(squares, ahead)
        mean_square = total[:, None] / model_width
        normed = (mixed_float * lax.rsqrt(mean_square + NORM_EPS) * norm_gain).astype(BF)

    with jax.named_scope("gather_tokens"):
        near = jnp.concatenate([normed, xor_x(normed, 1)], axis=1)
        far = jnp.concatenate([xor_x(normed, 2), xor_x(normed, 3)], axis=1)
        along_x = jnp.stack([near, far])
        token_pieces = []
        for ahead in range(NY):
            mine = along_x if ahead == 0 else from_y(along_x, ahead)
            token_pieces += [mine, swap_core(mine)]

    with jax.named_scope("gate_up"):
        partial_hidden = vmem_call(
            gate_up_kernel,
            jax.ShapeDtypeStruct((NZ, 2, 2 * CAP, hidden), BF),
            [SMEM] + [HBM] * 8 + [VMEM] * 2,
            [
                pltpu.VMEM((NZ, 2 * rows, 2 * columns), BF),
                pltpu.VMEM((2, NZ, 2 * CAP, 2 * columns), BF),
                pltpu.SemaphoreType.DMA((16,)),
            ],
            4 * 10**9,
            "gate_up",
        )(z.reshape(1), *token_pieces, place, up_weight)

    with jax.named_scope("sum_hidden"):
        ahead_in = [to_z(partial_hidden[4, 0], 1), None]
        back_in = [None, to_z(partial_hidden[4, 1], -1)]
        for step in (3, 2, 1):
            for e in (1, 0):
                out = partial_hidden[step, e]
                if ahead_in[e] is not None:
                    out = plus(out, ahead_in[e])
                ahead_in[e] = to_z(out, 1)
                out = partial_hidden[NZ - step, 1 - e]
                if back_in[1 - e] is not None:
                    out = plus(out, back_in[1 - e])
                back_in[1 - e] = to_z(out, -1)
        acts = []
        for e in range(2):
            full = partial_hidden[0, e].astype(F32) + ahead_in[e].astype(F32)
            full = full + back_in[e].astype(F32)
            acts.append((jax.nn.silu(full[:, :half_hidden]) * full[:, half_hidden:]).astype(BF))

    with jax.named_scope("gather_hidden"):
        chunks = {0: acts}
        for step in (1, 2, 3):
            chunks[-step] = [to_z(chunks[1 - step][e], 1) for e in range(2)]
            chunks[step] = [to_z(chunks[step - 1][e], -1) for e in range(2)]
        chunks[4] = [to_z(chunks[-3][0], 1), to_z(chunks[3][1], -1)]

    with jax.named_scope("down"):
        routed = jnp.zeros((rows, 2 * columns), F32)
        for step in (0, -1, 1, -2, 2, -3, 3, 4):
            chunk = (z + step) % NZ
            own_rows, other_rows = vmem_call(
                down_kernel,
                (jax.ShapeDtypeStruct((rows, 2 * columns), BF),) * 2,
                [VMEM] * 5,
                [],
                10**9,
                "down",
            )(
                *chunks[step],
                low_weight,
                lax.dynamic_index_in_dim(place, chunk, 0, keepdims=False),
                lax.dynamic_index_in_dim(gain, chunk, 0, keepdims=False),
            )
            both = plus(own_rows, swap_core(other_rows))
            routed = routed + to_owner(both, step).astype(F32)
        routed = routed[:, :columns] + xor_x(routed[:, columns:].astype(BF), 1).astype(F32)
        return (mixed_float + routed).astype(BF)


def solution(mesh):
    fine = Mesh(mesh.devices.reshape(2, NY, 2, 2, NZ), AXES)
    return jax.shard_map(
        body,
        mesh=fine,
        in_specs=(
            P(SEQ, EXP),
            P(SEQ, EXP),
            P(SEQ, EXP),
            P(SEQ, None),
            P(SEQ, None),
            P(EXP, None, None),
            P(EXP, None, None),
            P(EXP, None),
            P(EXP),
            P(SEQ, EXP, None),
            P(SEQ, None, EXP),
            P(SEQ, None),
            P(SEQ, None),
        ),
        out_specs=P(SEQ, EXP),
        check_vma=False,
    )
```

```python
import functools
import math

import jax
import jax.numpy as jnp
from jax import lax
from jax.experimental import pallas as pl
from jax.experimental.pallas import tpu as pltpu
from jax.sharding import Mesh, PartitionSpec as P

CAP = 48
NORM_EPS = 1e-06
BF = jnp.bfloat16
F32 = jnp.float32

AXES = ("xh", "y", "core", "xl", "z")
SEQ = ("xh", "y", "core")
EXP = ("xl", "z")
NX, NY, NZ = 4, 4, 8


def xor_x(value, bits):
    return lax.ppermute(value, ("xh", "xl"), [(s, s ^ bits) for s in range(NX)])


def from_y(value, ahead):
    return lax.ppermute(value, "y", [(s, (s - ahead) % NY) for s in range(NY)])


def swap_core(value):
    return lax.ppermute(value, "core", [(0, 1), (1, 0)])


def to_z(value, ahead):
    return lax.ppermute(value, "z", [(s, (s + ahead) % NZ) for s in range(NZ)])


def after(value, *earlier):
    return lax.optimization_barrier((value, *earlier))[0]


def plus(a, b):
    return (a.astype(F32) + b.astype(F32)).astype(BF)


VMEM = pl.BlockSpec(memory_space=pltpu.VMEM)
SMEM = pl.BlockSpec(memory_space=pltpu.SMEM)
ANY = pl.BlockSpec(memory_space=pl.ANY)


def vmem_call(kernel, out_shape, in_specs, scratch, flops, name):
    return pl.pallas_call(
        kernel,
        out_shape=out_shape,
        in_specs=in_specs,
        out_specs=jax.tree.map(lambda _: VMEM, out_shape),
        scratch_shapes=scratch,
        compiler_params=pltpu.CompilerParams(vmem_limit_bytes=48 * 2**20),
        cost_estimate=pl.CostEstimate(flops=flops, bytes_accessed=8 * 2**20, transcendentals=0),
        name=name,
    )


def load_all(sources, targets, sems):
    copies = [
        pltpu.make_async_copy(source, target, sems.at[i])
        for i, (source, target) in enumerate(zip(sources, targets))
    ]
    for copy in copies:
        copy.start()
    return copies


def pack_kernel(latent_in, rope_in, ids_in, gains_in, out_ref, *scratch):
    latent_ref, rope_ref, ids_ref, gains_ref, notes_ref, sems = scratch
    width, rope, topk = latent_ref.shape[1], rope_ref.shape[0], ids_ref.shape[0]
    copies = load_all(
        (latent_in, rope_in, ids_in, gains_in), (latent_ref, rope_ref, ids_ref, gains_ref), sems
    )
    notes_ref[rope:] = jnp.zeros((notes_ref.shape[0] - rope, notes_ref.shape[1]), F32)
    notes_ref[rope : rope + 8] = jnp.full((8, notes_ref.shape[1]), -1.0, F32)
    for copy in copies:
        copy.wait()
    notes_ref[:rope] = rope_ref[...].astype(F32)
    notes_ref[rope : rope + topk] = ids_ref[...].astype(F32)
    rest = gains_ref[...]
    for part in range(1, 4):
        rounded = rest.astype(BF).astype(F32)
        notes_ref[rope + 8 * part : rope + 8 * part + topk] = rounded
        rest = rest - rounded
    out_ref[:, :width] = latent_ref[...]
    out_ref[:, width:] = jnp.transpose(notes_ref[...]).astype(BF)


def score_pieces(score_scale, heads, spot_ref, q_ref, places_ref, kv_ref, copies, *refs):
    scores_ref, notes_ref = refs
    rows = q_ref.shape[0] // heads
    keys = kv_ref.shape[0] // len(copies)
    width = kv_ref.shape[1] - 128
    query_places = spot_ref[0] + lax.broadcasted_iota(jnp.int32, (rows, keys), 0)
    tops = [None] * heads
    for p, copy in enumerate(copies):
        copy.wait()
        here = slice(p * keys, (p + 1) * keys)
        notes_ref[p] = kv_ref[here, width:]
        allowed = places_ref[:, here] <= query_places
        scores = lax.dot_general(
            q_ref[...], kv_ref[here], (((1,), (1,)), ((), ())), preferred_element_type=F32
        )
        for h in range(heads):
            lines = slice(h * rows, (h + 1) * rows)
            masked = jnp.where(allowed, scores[lines] * score_scale, -1e30)
            scores_ref[lines, here] = masked
            top = jnp.max(masked, axis=1, keepdims=True)
            tops[h] = top if p == 0 else jnp.maximum(tops[h], top)
    return tops


def weigh_pieces(tops, pieces, scores_ref, weights_ref):
    heads = len(tops)
    rows, keys = scores_ref.shape[0] // heads, scores_ref.shape[1] // pieces
    masses = [None] * heads
    for h in range(heads):
        lines = slice(h * rows, (h + 1) * rows)
        for p in range(pieces):
            here = slice(p * keys, (p + 1) * keys)
            weights = jnp.exp(scores_ref[lines, here] - tops[h])
            mass = jnp.sum(weights, axis=1, keepdims=True)
            masses[h] = mass if p == 0 else masses[h] + mass
            weights_ref[lines, here] = weights.astype(BF)
    return masses


def attention_start_kernel(score_scale, pieces, heads, spot_ref, q_in, *refs):
    kv_refs = refs[:pieces]
    places_ref, total_ref, top_ref, mass_ref, notes_ref = refs[pieces : pieces + 5]
    q_ref, kv_ref, scores_ref, weights_ref, sems = refs[pieces + 5 :]
    keys = kv_refs[0].shape[0]
    copies = load_all(
        (q_in, *kv_refs),
        (q_ref, *[kv_ref.at[pl.ds(p * keys, keys)] for p in range(pieces)]),
        sems,
    )
    copies[0].wait()
    tops = score_pieces(
        score_scale, heads, spot_ref, q_ref, places_ref, kv_ref, copies[1:], scores_ref, notes_ref
    )
    masses = weigh_pieces(tops, pieces, scores_ref, weights_ref)
    width = total_ref.shape[1]
    total_ref[...] = jnp.dot(weights_ref[...], kv_ref[:, :width], preferred_element_type=F32)
    rows = q_ref.shape[0] // heads
    for h in range(heads):
        lines = slice(h * rows, (h + 1) * rows)
        top_ref[lines] = jnp.broadcast_to(tops[h], (rows, 128))
        mass_ref[lines] = jnp.broadcast_to(masses[h], (rows, 128))


def attention_kernel(score_scale, pieces, spot_ref, q_in, *refs):
    kv_refs = refs[:pieces]
    places_ref, before_ref, top_ref, mass_ref, lift_in, weight_in, out_ref, notes_ref = refs[
        pieces : pieces + 8
    ]
    q_ref, kv_ref, lift_ref, mix_ref, scores_ref, weights_ref, values_ref, sems = refs[pieces + 8 :]
    heads, width, value_width = lift_ref.shape
    rows = q_ref.shape[0] // heads
    keys = kv_refs[0].shape[0]
    copies = load_all(
        (q_in, *kv_refs, lift_in, weight_in),
        (q_ref, *[kv_ref.at[pl.ds(p * keys, keys)] for p in range(pieces)], lift_ref, mix_ref),
        sems,
    )
    copies[0].wait()
    tops = score_pieces(
        score_scale,
        heads,
        spot_ref,
        q_ref,
        places_ref,
        kv_ref,
        copies[1 : 1 + pieces],
        scores_ref,
        notes_ref,
    )
    shrink = []
    for h in range(heads):
        old = top_ref[h * rows : (h + 1) * rows, :1]
        tops[h] = jnp.maximum(tops[h], old)
        shrink.append(jnp.exp(old - tops[h]))
    masses = weigh_pieces(tops, pieces, scores_ref, weights_ref)
    total = jnp.dot(weights_ref[...], kv_ref[:, :width], preferred_element_type=F32)
    copies[1 + pieces].wait()
    for h in range(heads):
        lines = slice(h * rows, (h + 1) * rows)
        mass = masses[h] + mass_ref[lines, :1] * shrink[h]
        attended = ((total[lines] + before_ref[lines] * shrink[h]) / mass).astype(BF)
        values_ref[:, h * value_width : (h + 1) * value_width] = jnp.dot(
            attended, lift_ref[h], preferred_element_type=F32
        ).astype(BF)
    copies[2 + pieces].wait()
    two = out_ref.shape[1]
    column = two // 2
    for i in range(NZ // 2):
        parts = []
        for half in range(2):
            first = (half * NZ // 2 + i) * two
            part = jnp.dot(
                values_ref[...], mix_ref[:, first : first + two], preferred_element_type=F32
            )
            parts.append(jnp.transpose(part).astype(BF))
        for odd in range(2):
            step = (2 * i + odd - spot_ref[1] + NZ) % NZ
            for half in range(2):
                out_ref[step, half * column : (half + 1) * column] = parts[half][
                    odd * column : (odd + 1) * column
                ]


def routing_kernel(first, spot_ref, early_ref, late_ref, place_ref, gain_ref, masks_ref):
    rows = place_ref.shape[1]
    blocks = [early_ref[p] for p in range(early_ref.shape[0])]
    blocks += [late_ref[p] for p in range(late_ref.shape[0])]
    for p, block in enumerate(blocks):
        notes = jnp.transpose(block.astype(F32))[first : first + 32]
        for jx in range(2):
            block = notes[:, jx * rows : (jx + 1) * rows]
            named = block[:8] == spot_ref[0].astype(F32)
            gains = block[8:16] + block[16:24] + block[24:32]
            index = (jx * NY + p // 2) * 2 + p % 2
            masks_ref[index : index + 1] = jnp.max(
                jnp.where(named, 1.0, 0.0), axis=0, keepdims=True
            )
            gain_ref[index : index + 1] = jnp.sum(
                jnp.where(named, gains, 0.0), axis=0, keepdims=True
            )
    earlier = lax.broadcasted_iota(jnp.int32, (rows, rows), 0) < lax.broadcasted_iota(
        jnp.int32, (rows, rows), 1
    )
    mask = masks_ref[...]
    ranks = jnp.dot(
        mask.astype(BF), jnp.where(earlier, 1.0, 0.0).astype(BF), preferred_element_type=F32
    )
    place_ref[...] = jnp.where(mask > 0, ranks, -1.0).astype(jnp.int32)


def slot_matrix(places):
    ranks = lax.broadcasted_iota(jnp.int32, (CAP, places.shape[1]), 0)
    return jnp.where(ranks == places, 1.0, 0.0)


def gate_up_kernel(steps, spot_ref, *refs):
    token_refs = refs[:8]
    place_ref, gain_ref, keep_ref, first_ref, second_ref = refs[8:13]
    out_refs = refs[13 : 13 + 2 * len(steps)]
    tokens_ref, weight_ref, rows_ref, sems = refs[13 + 2 * len(steps) :]
    tokens = token_refs[0].shape[2]
    columns, width = keep_ref.shape[1:]
    copies = []
    for piece in range(8):
        for jx in range(2):
            copies.append(
                pltpu.make_async_copy(
                    token_refs[piece].at[jx],
                    tokens_ref.at[jx * NY + piece // 2, :, pl.ds(piece % 2 * tokens, tokens)],
                    sems.at[piece * 2 + jx],
                )
            )
    half = columns // 2
    mine = pl.multiple_of(spot_ref[1] * columns, columns)
    other = pl.multiple_of((1 - spot_ref[1]) * columns, columns)
    loads = [
        pltpu.make_async_copy(
            keep_ref.at[spot_ref[1]], weight_ref.at[pl.ds(mine, columns)], sems.at[16]
        ),
        pltpu.make_async_copy(first_ref, weight_ref.at[pl.ds(other, half)], sems.at[17]),
        pltpu.make_async_copy(second_ref, weight_ref.at[pl.ds(other + half, half)], sems.at[18]),
    ]
    for copy in copies + loads:
        copy.start()
    for copy in copies:
        copy.wait()
    for i, step in enumerate(steps):
        chunk = (spot_ref[0] + step) % NZ
        empty = jnp.zeros((CAP, tokens), F32)
        first = slot_matrix(place_ref[pl.ds(chunk * 2, 1)])
        second = slot_matrix(place_ref[pl.ds(chunk * 2 + 1, 1)])
        picks = jnp.concatenate(
            [
                jnp.concatenate([first, empty], axis=1),
                jnp.concatenate([empty, second], axis=1),
            ],
            axis=0,
        ).astype(BF)
        rows = lax.dot_general(
            picks, tokens_ref[chunk], (((1,), (1,)), ((), ())), preferred_element_type=F32
        )
        squares = jnp.sum(rows * rows, axis=1, keepdims=True)
        squares = jnp.broadcast_to(squares, (2 * CAP, 128)).astype(BF)
        out_refs[2 * i][:, width:] = squares[:CAP]
        out_refs[2 * i + 1][:, width:] = squares[CAP:]
        rows_ref[i] = (rows * gain_ref[...]).astype(BF)
    for load in loads:
        load.wait()
    tile = 1536
    rows = rows_ref[...].reshape(len(steps) * 2 * CAP, 2 * columns)
    for n in range(0, width, tile):
        hidden = jnp.dot(
            rows, weight_ref[:, n : n + tile], preferred_element_type=F32
        ).astype(BF)
        for i in range(2 * len(steps)):
            out_refs[i][:, n : n + tile] = hidden[i * CAP : (i + 1) * CAP]


def down_kernel(steps, spot_ref, *refs):
    count = len(steps)
    act_refs = refs[: 2 * count]
    keep_ref, taken_ref, place_ref, gain_ref, own_ref, other_ref = refs[2 * count : 2 * count + 6]
    acts_ref, weight_ref, outs_ref, sems = refs[2 * count + 6 :]
    spread = 128
    copies = load_all(
        (keep_ref.at[spot_ref[1]], taken_ref, *act_refs),
        (
            weight_ref.at[0],
            weight_ref.at[1],
            *[
                acts_ref.at[pl.ds(i // 2 * spread + i % 2 * CAP, CAP)]
                for i in range(2 * count)
            ],
        ),
        sems,
    )
    left = spread - 2 * CAP
    for i in range(count):
        acts_ref[i * spread + 2 * CAP : (i + 1) * spread] = jnp.zeros(
            (left, acts_ref.shape[1]), BF
        )
    picks, gains = [], []
    tokens = place_ref.shape[1]
    empty = jnp.zeros((CAP, tokens), F32)
    for i in range(count):
        chunk = (spot_ref[0] + steps[i] + NZ) % NZ
        first = slot_matrix(place_ref[pl.ds(chunk * 2, 1)])
        second = slot_matrix(place_ref[pl.ds(chunk * 2 + 1, 1)])
        pick = [
            jnp.concatenate([first, empty], axis=1),
            jnp.concatenate([empty, second], axis=1),
            jnp.zeros((left, 2 * tokens), F32),
        ]
        picks.append(jnp.concatenate(pick, axis=0).astype(BF))
        gains.append([gain_ref[pl.ds(chunk * 2 + c, 1)] for c in range(2)])
    for copy in copies:
        copy.wait()
    for half in range(2):
        outs_ref[half] = lax.dot_general(
            weight_ref[half], acts_ref[...], (((1,), (1,)), ((), ())), preferred_element_type=F32
        ).astype(BF)
    for i in range(count):
        for half in range(2):
            rows = jnp.dot(
                outs_ref[half, :, i * spread : (i + 1) * spread],
                picks[i],
                preferred_element_type=F32,
            )
            own_ref[half, i] = (rows[:, :tokens] * gains[i][0]).astype(BF)
            other_ref[half, i] = (rows[:, tokens:] * gains[i][1]).astype(BF)


def merge_kernel(groups, z_ref, *refs):
    for g, steps in enumerate(groups):
        own_ref, taken_ref = refs[2 * g : 2 * g + 2]
        for i, step in enumerate(steps):
            chunk = (z_ref[0] + step + NZ) % NZ
            for half in range(2):
                total = plus(own_ref[half, i], taken_ref[half, i])
                for jx in range(2):
                    out_ref = refs[2 * len(groups) + 2 * jx + half]

                    @pl.when(chunk // NY == jx)
                    def _():
                        out_ref[chunk % NY] = total


def body(
    residual,
    query_nope,
    query_rope,
    latent,
    key_rope,
    key_lift,
    value_lift,
    out_weight,
    norm_gain,
    gate_up_weight,
    down_weight,
    route_ids,
    route_weights,
):
    rows, columns = residual.shape
    heads, width, nope = key_lift.shape
    rope = key_rope.shape[1]
    topk = route_ids.shape[1]
    hidden = down_weight.shape[1]
    model_width = out_weight.shape[1]
    score_scale = 1.0 / math.sqrt(nope + rope)
    xh, y, core = lax.axis_index("xh"), lax.axis_index("y"), lax.axis_index("core")
    xl, z = lax.axis_index("xl"), lax.axis_index("z")
    shard = (xh * NY + y) * 2 + core

    with jax.named_scope("gather_keys"):
        packed = vmem_call(
            pack_kernel,
            jax.ShapeDtypeStruct((rows, width + 128), BF),
            [ANY] * 4,
            [
                pltpu.VMEM((rows, width), BF),
                pltpu.VMEM((rope, rows), BF),
                pltpu.VMEM((topk, rows), jnp.int32),
                pltpu.VMEM((topk, rows), F32),
                pltpu.VMEM((128, rows), F32),
                pltpu.SemaphoreType.DMA((4,)),
            ],
            10**6,
            "pack",
        )(latent, key_rope.T, route_ids.T, route_weights.T)
        along_x = jnp.concatenate([packed, xor_x(packed, 3)], axis=0)
        pieces = []
        for ahead in range(NY):
            mine = along_x if ahead == 0 else from_y(along_x, ahead)
            pieces += [mine, swap_core(mine)]

    with jax.named_scope("swap_weights"):
        up, gain_own, residual_own = after((gate_up_weight, norm_gain, residual.T), along_x)
        half_columns = columns // 2
        up_gives = [
            lax.dynamic_slice(
                up, (1 - xl, i * half_columns, 0), (1, half_columns, 2 * hidden)
            ).reshape(half_columns, 2 * hidden)
            for i in range(2)
        ]
        up_takens = [xor_x(give, 1) for give in up_gives]

        def in_order(own, other):
            return jnp.where(
                xl == 0, jnp.concatenate([own, other]), jnp.concatenate([other, own])
            )

        gain_columns = in_order(gain_own, xor_x(gain_own, 1))[None, :]
        residual_columns = in_order(residual_own, xor_x(residual_own, 1))

    with jax.named_scope("attention"):
        query_heads = query_nope.reshape(rows, heads, nope)
        query_latent = jnp.einsum(
            "thn,hln->htl", query_heads, key_lift, preferred_element_type=F32
        ).astype(BF)
        query_rotary = jnp.transpose(query_rope.reshape(rows, heads, rope), (1, 0, 2))
        queries = jnp.concatenate(
            [query_latent, query_rotary, jnp.zeros((heads, rows, 128 - rope), BF)], axis=2
        ).reshape(heads * rows, width + 128)
        starts = []
        for ahead in range(NY):
            for flip in range(2):
                for jx in range(2):
                    starts.append(((xh ^ jx) * NY + (y + ahead) % NY) * 2 + (core ^ flip))
        places = jnp.stack(starts)[:, None] * rows + jnp.arange(rows, dtype=jnp.int32)[None, :]
        places = places.reshape(1, -1)
        spot = jnp.stack([shard * rows, z])
        queries = after(queries, *up_gives, gain_columns, residual_columns)
        lines = heads * rows
        count = len(pieces) // 2
        keys = count * 2 * rows
        state = [
            pltpu.VMEM((lines, width + 128), BF),
            pltpu.VMEM((keys, width + 128), BF),
        ]
        sheets = [pltpu.VMEM((lines, keys), F32), pltpu.VMEM((lines, keys), BF)]
        total, top, mass, early_notes = vmem_call(
            functools.partial(attention_start_kernel, score_scale, count, heads),
            (
                jax.ShapeDtypeStruct((lines, width), F32),
                jax.ShapeDtypeStruct((lines, 128), F32),
                jax.ShapeDtypeStruct((lines, 128), F32),
                jax.ShapeDtypeStruct((count, 2 * rows, 128), BF),
            ),
            [SMEM] + [ANY] * (1 + count) + [VMEM],
            state + sheets + [pltpu.SemaphoreType.DMA((count + 1,))],
            2 * 10**9,
            "attention_start",
        )(spot, queries, *pieces[:count], places[:, :keys])
        partial_mix, late_notes = vmem_call(
            functools.partial(attention_kernel, score_scale, count),
            (
                jax.ShapeDtypeStruct((NZ, 2 * columns, rows), BF),
                jax.ShapeDtypeStruct((count, 2 * rows, 128), BF),
            ),
            [SMEM] + [ANY] * (1 + count) + [VMEM] * 4 + [ANY] * 2,
            state
            + [
                pltpu.VMEM(value_lift.shape, BF),
                pltpu.VMEM(out_weight.shape, BF),
            ]
            + sheets
            + [
                pltpu.VMEM((rows, heads * value_lift.shape[2]), BF),
                pltpu.SemaphoreType.DMA((count + 3,)),
            ],
            3 * 10**9,
            "attention",
        )(
            spot,
            queries,
            *pieces[count:],
            places[:, keys:],
            total,
            top,
            mass,
            value_lift,
            out_weight,
        )

    with jax.named_scope("routing"):
        place, gain = vmem_call(
            functools.partial(routing_kernel, rope),
            (
                jax.ShapeDtypeStruct((2 * NZ, rows), jnp.int32),
                jax.ShapeDtypeStruct((2 * NZ, rows), F32),
            ),
            [SMEM] + [VMEM] * 2,
            [pltpu.VMEM((2 * NZ, rows), F32)],
            10**8,
            "routing",
        )((2 * shard + xl).reshape(1), early_notes, late_notes)

    with jax.named_scope("sum_mix"):
        partial_mix = after(partial_mix, up_takens[0])
        far_in = to_z(partial_mix[4], 4)
        ahead_in, back_in = to_z(partial_mix[3], 1), to_z(partial_mix[5], -1)
        partial_mix = after(partial_mix, place, gain)
        for step in (2, 1):
            ahead_out = plus(partial_mix[step], ahead_in)
            back_out = plus(partial_mix[NZ - step], back_in)
            if step == 1:
                ahead_out = after(ahead_out, up_takens[1])
            ahead_in, back_in = to_z(ahead_out, 1), to_z(back_out, -1)
        mix = partial_mix[0].astype(F32) + far_in.astype(F32)
        mix = (mix + ahead_in.astype(F32) + back_in.astype(F32)).astype(BF)
        mix = mix.astype(F32) + xor_x(mix, 1).astype(F32)
        mixed = (residual_columns.astype(F32) + mix).astype(BF)

    with jax.named_scope("gather_tokens"):
        along_x = jnp.stack([mixed, xor_x(mixed, 3)])
        token_pieces = []
        for ahead in range(NY):
            mine = along_x if ahead == 0 else from_y(along_x, ahead)
            token_pieces += [mine, swap_core(mine)]

    with jax.named_scope("swap_weights"):
        down = after(jnp.swapaxes(down_weight, 1, 2), *token_pieces)
        down_taken = xor_x(lax.dynamic_index_in_dim(down, 1 - xl, 0, keepdims=False), 1)

    with jax.named_scope("gate_up"):
        wide = 2 * hidden + 128
        spot = jnp.stack([z, xl])
        partial_hidden = {}
        for steps in ((4, 3, 5), (6, 2, 7, 1, 0)):
            flat = vmem_call(
                functools.partial(gate_up_kernel, steps),
                (jax.ShapeDtypeStruct((CAP, wide), BF),) * (2 * len(steps)),
                [SMEM] + [ANY] * 8 + [VMEM] * 2 + [ANY] * 3,
                [
                    pltpu.VMEM((NZ, 2 * columns, 2 * rows), BF),
                    pltpu.VMEM((2 * columns, 2 * hidden), BF),
                    pltpu.VMEM((len(steps), 2 * CAP, 2 * columns), BF),
                    pltpu.SemaphoreType.DMA((19,)),
                ],
                4 * 10**9,
                "gate_up",
            )(spot, *token_pieces, place, gain_columns, gate_up_weight, *up_takens)
            partial_hidden.update({k: flat[2 * i : 2 * i + 2] for i, k in enumerate(steps)})

    with jax.named_scope("sum_hidden"):
        ahead_in = [to_z(partial_hidden[4][0], 1), None]
        back_in = [None, to_z(partial_hidden[4][1], -1)]
        for step in (3, 2, 1):
            for c in (1, 0):
                out = partial_hidden[step][c]
                if ahead_in[c] is not None:
                    out = plus(out, ahead_in[c])
                ahead_in[c] = to_z(out, 1)
                out = partial_hidden[NZ - step][1 - c]
                if back_in[1 - c] is not None:
                    out = plus(out, back_in[1 - c])
                back_in[1 - c] = to_z(out, -1)
        acts = []
        for c in range(2):
            full = partial_hidden[0][c].astype(F32) + ahead_in[c].astype(F32)
            full = full + back_in[c].astype(F32)
            factor = lax.rsqrt(full[:, 2 * hidden : 2 * hidden + 1] / model_width + NORM_EPS)
            full = full * factor
            acts.append((jax.nn.silu(full[:, :hidden]) * full[:, hidden : 2 * hidden]).astype(BF))

    with jax.named_scope("gather_hidden"):
        chunks = {0: acts}
        for step in (1, 2, 3):
            chunks[-step] = [to_z(chunks[1 - step][c], 1) for c in range(2)]
            chunks[step] = [to_z(chunks[step - 1][c], -1) for c in range(2)]
        chunks[4] = [to_z(chunks[-3][0], 1), to_z(chunks[3][1], -1)]

    with jax.named_scope("down"):
        groups = ((0, -1, 1, -2, 2), (-3, 3, 4))
        parts = []
        for steps in groups:
            count = len(steps)
            own_rows, other_rows = vmem_call(
                functools.partial(down_kernel, steps),
                (jax.ShapeDtypeStruct((2, count, columns, rows), BF),) * 2,
                [SMEM] + [ANY] * (2 * count + 2) + [VMEM] * 2,
                [
                    pltpu.VMEM((count * 128, hidden), BF),
                    pltpu.VMEM((2, columns, hidden), BF),
                    pltpu.VMEM((2, columns, count * 128), BF),
                    pltpu.SemaphoreType.DMA((2 * count + 2,)),
                ],
                2 * 10**9,
                "down",
            )(
                spot,
                *[chunks[step][c] for step in steps for c in range(2)],
                down,
                down_taken,
                place,
                gain,
            )
            parts += [own_rows, swap_core(other_rows)]

    with jax.named_scope("return_rows"):
        gives = vmem_call(
            functools.partial(merge_kernel, groups),
            (jax.ShapeDtypeStruct((NY, columns, rows), BF),) * 4,
            [SMEM] + [VMEM] * 4,
            [],
            10**7,
            "merge",
        )(z.reshape(1), *parts)
        total = gives[0].astype(F32)
        for bits in (1, 2, 3):
            total = total + xor_x(gives[bits], bits).astype(F32)
        routed = total[0]
        for ahead in range(1, NY):
            routed = routed + from_y(total[ahead].astype(BF), -ahead).astype(F32)
        mine = lax.dynamic_slice_in_dim(mixed, xl * columns, columns, axis=0)
        return (mine.astype(F32) + routed).astype(BF).T


def solution(mesh):
    fine = Mesh(mesh.devices.reshape(2, NY, 2, 2, NZ), AXES)
    return jax.shard_map(
        body,
        mesh=fine,
        in_specs=(
            P(SEQ, EXP),
            P(SEQ, EXP),
            P(SEQ, EXP),
            P(SEQ, None),
            P(SEQ, None),
            P(EXP, None, None),
            P(EXP, None, None),
            P(EXP, None),
            P(EXP),
            P(SEQ, EXP, None),
            P(SEQ, None, EXP),
            P(SEQ, None),
            P(SEQ, None),
        ),
        out_specs=P(SEQ, EXP),
        check_vma=False,
    )
```

```python
import functools
import math

import jax
import jax.numpy as jnp
from jax import lax
from jax.experimental import pallas as pl
from jax.experimental.pallas import tpu as pltpu
from jax.sharding import Mesh, PartitionSpec as P

CAP = 48
NORM_EPS = 1e-06
BF = jnp.bfloat16
F32 = jnp.float32

AXES = ("xh", "y", "core", "xl", "z")
SEQ = ("xh", "y", "core")
EXP = ("xl", "z")
NX, NY, NZ = 4, 4, 8


def xor_x(value, bits):
    return lax.ppermute(value, ("xh", "xl"), [(s, s ^ bits) for s in range(NX)])


def from_y(value, ahead):
    return lax.ppermute(value, "y", [(s, (s - ahead) % NY) for s in range(NY)])


def swap_core(value):
    return lax.ppermute(value, "core", [(0, 1), (1, 0)])


def to_z(value, ahead):
    return lax.ppermute(value, "z", [(s, (s + ahead) % NZ) for s in range(NZ)])


def after(value, *earlier):
    return lax.optimization_barrier((value, *earlier))[0]


def plus(a, b):
    return (a.astype(F32) + b.astype(F32)).astype(BF)


VMEM = pl.BlockSpec(memory_space=pltpu.VMEM)
SMEM = pl.BlockSpec(memory_space=pltpu.SMEM)
ANY = pl.BlockSpec(memory_space=pl.ANY)


def vmem_call(kernel, out_shape, in_specs, scratch, flops, name, grant=24):
    return pl.pallas_call(
        kernel,
        out_shape=out_shape,
        in_specs=in_specs,
        out_specs=jax.tree.map(lambda _: VMEM, out_shape),
        scratch_shapes=scratch,
        compiler_params=pltpu.CompilerParams(vmem_limit_bytes=grant * 2**20),
        cost_estimate=pl.CostEstimate(flops=flops, bytes_accessed=flops // 256, transcendentals=0),
        name=name,
    )


def load_all(sources, targets, sems):
    copies = [
        pltpu.make_async_copy(source, target, sems.at[i])
        for i, (source, target) in enumerate(zip(sources, targets))
    ]
    for copy in copies:
        copy.start()
    return copies


def pack_kernel(latent_in, rope_in, ids_in, gains_in, out_ref, *scratch):
    latent_ref, rope_ref, ids_ref, gains_ref, notes_ref, sems = scratch
    width, rope, topk = latent_ref.shape[1], rope_ref.shape[0], ids_ref.shape[0]
    copies = load_all(
        (latent_in, rope_in, ids_in, gains_in), (latent_ref, rope_ref, ids_ref, gains_ref), sems
    )
    notes_ref[rope:] = jnp.zeros((notes_ref.shape[0] - rope, notes_ref.shape[1]), F32)
    notes_ref[rope : rope + 8] = jnp.full((8, notes_ref.shape[1]), -1.0, F32)
    for copy in copies:
        copy.wait()
    notes_ref[:rope] = rope_ref[...].astype(F32)
    notes_ref[rope : rope + topk] = ids_ref[...].astype(F32)
    rest = gains_ref[...]
    for part in range(1, 4):
        rounded = rest.astype(BF).astype(F32)
        notes_ref[rope + 8 * part : rope + 8 * part + topk] = rounded
        rest = rest - rounded
    out_ref[:, :width] = latent_ref[...]
    out_ref[:, width:] = jnp.transpose(notes_ref[...]).astype(BF)


def score_pieces(score_scale, heads, spot_ref, q_ref, places_ref, kv_refs, scores_ref, notes_ref):
    rows = q_ref.shape[0] // heads
    keys = kv_refs[0].shape[0]
    width = kv_refs[0].shape[1] - 128
    query_places = spot_ref[0] + lax.broadcasted_iota(jnp.int32, (rows, keys), 0)
    tops = [None] * heads
    for p, kv_ref in enumerate(kv_refs):
        here = slice(p * keys, (p + 1) * keys)
        notes_ref[p] = kv_ref[:, width:]
        allowed = places_ref[:, here] <= query_places
        scores = lax.dot_general(
            q_ref[...], kv_ref[...], (((1,), (1,)), ((), ())), preferred_element_type=F32
        )
        for h in range(heads):
            lines = slice(h * rows, (h + 1) * rows)
            masked = jnp.where(allowed, scores[lines] * score_scale, -1e30)
            scores_ref[lines, here] = masked
            for lane in range(0, keys, 128):
                part = masked[:, lane : lane + 128]
                tops[h] = part if tops[h] is None else jnp.maximum(tops[h], part)
    return [jnp.max(top, axis=1, keepdims=True) for top in tops]


def weigh_pieces(tops, pieces, scores_ref, weights_ref):
    heads = len(tops)
    rows, keys = scores_ref.shape[0] // heads, scores_ref.shape[1] // pieces
    masses = [None] * heads
    for h in range(heads):
        lines = slice(h * rows, (h + 1) * rows)
        for p in range(pieces):
            here = slice(p * keys, (p + 1) * keys)
            weights = jnp.exp(scores_ref[lines, here] - tops[h])
            for lane in range(0, keys, 128):
                part = weights[:, lane : lane + 128]
                masses[h] = part if masses[h] is None else masses[h] + part
            weights_ref[lines, here] = weights.astype(BF)
    return [jnp.sum(mass, axis=1, keepdims=True) for mass in masses]


def attention_start_kernel(score_scale, pieces, heads, spot_ref, q_ref, *refs):
    kv_refs = refs[:pieces]
    places_ref, total_ref, top_ref, mass_ref, notes_ref = refs[pieces : pieces + 5]
    kv_ref, scores_ref, weights_ref, sems = refs[pieces + 5 :]
    keys = kv_refs[0].shape[0]
    copies = load_all(kv_refs, [kv_ref.at[pl.ds(p * keys, keys)] for p in range(pieces)], sems)
    tops = score_pieces(
        score_scale, heads, spot_ref, q_ref, places_ref, kv_refs, scores_ref, notes_ref
    )
    masses = weigh_pieces(tops, pieces, scores_ref, weights_ref)
    for copy in copies:
        copy.wait()
    width = total_ref.shape[1]
    total_ref[...] = jnp.dot(weights_ref[...], kv_ref[:, :width], preferred_element_type=F32)
    rows = q_ref.shape[0] // heads
    for h in range(heads):
        lines = slice(h * rows, (h + 1) * rows)
        top_ref[lines] = jnp.broadcast_to(tops[h], (rows, 128))
        mass_ref[lines] = jnp.broadcast_to(masses[h], (rows, 128))


def attention_kernel(score_scale, pieces, spot_ref, q_ref, *refs):
    kv_refs = refs[:pieces]
    places_ref, before_ref, top_ref, mass_ref, lift_in, weight_in, out_ref, notes_ref = refs[
        pieces : pieces + 8
    ]
    kv_ref, lift_ref, mix_ref, scores_ref, weights_ref, values_ref, sems = refs[pieces + 8 :]
    heads, width, value_width = lift_ref.shape
    rows = q_ref.shape[0] // heads
    keys = kv_refs[0].shape[0]
    copies = load_all(
        (*kv_refs, lift_in, weight_in),
        (*[kv_ref.at[pl.ds(p * keys, keys)] for p in range(pieces)], lift_ref, mix_ref),
        sems,
    )
    tops = score_pieces(
        score_scale, heads, spot_ref, q_ref, places_ref, kv_refs, scores_ref, notes_ref
    )
    shrink = []
    for h in range(heads):
        old = top_ref[h * rows : (h + 1) * rows, :1]
        tops[h] = jnp.maximum(tops[h], old)
        shrink.append(jnp.exp(old - tops[h]))
    masses = weigh_pieces(tops, pieces, scores_ref, weights_ref)
    for copy in copies[: pieces + 1]:
        copy.wait()
    total = jnp.dot(weights_ref[...], kv_ref[:, :width], preferred_element_type=F32)
    for h in range(heads):
        lines = slice(h * rows, (h + 1) * rows)
        mass = masses[h] + mass_ref[lines, :1] * shrink[h]
        attended = ((total[lines] + before_ref[lines] * shrink[h]) / mass).astype(BF)
        values_ref[:, h * value_width : (h + 1) * value_width] = jnp.dot(
            attended, lift_ref[h], preferred_element_type=F32
        ).astype(BF)
    copies[pieces + 1].wait()
    two = out_ref.shape[1]
    column = two // 2
    for i in range(NZ // 2):
        parts = []
        for half in range(2):
            first = (half * NZ // 2 + i) * two
            part = jnp.dot(
                values_ref[...], mix_ref[:, first : first + two], preferred_element_type=F32
            )
            parts.append(jnp.transpose(part).astype(BF))
        for odd in range(2):
            step = (2 * i + odd - spot_ref[1] + NZ) % NZ
            for half in range(2):
                out_ref[step, half * column : (half + 1) * column] = parts[half][
                    odd * column : (odd + 1) * column
                ]


def routing_kernel(first, spot_ref, early_ref, late_ref, place_ref, gain_ref, masks_ref):
    rows = place_ref.shape[1]
    blocks = [early_ref[p] for p in range(early_ref.shape[0])]
    blocks += [late_ref[p] for p in range(late_ref.shape[0])]
    for p, block in enumerate(blocks):
        notes = jnp.transpose(block.astype(F32))[first : first + 32]
        for jx in range(2):
            block = notes[:, jx * rows : (jx + 1) * rows]
            named = block[:8] == spot_ref[0].astype(F32)
            gains = block[8:16] + block[16:24] + block[24:32]
            index = (jx * NY + p // 2) * 2 + p % 2
            masks_ref[index : index + 1] = jnp.max(
                jnp.where(named, 1.0, 0.0), axis=0, keepdims=True
            )
            gain_ref[index : index + 1] = jnp.sum(
                jnp.where(named, gains, 0.0), axis=0, keepdims=True
            )
    earlier = lax.broadcasted_iota(jnp.int32, (rows, rows), 0) < lax.broadcasted_iota(
        jnp.int32, (rows, rows), 1
    )
    mask = masks_ref[...]
    ranks = jnp.dot(
        mask.astype(BF), jnp.where(earlier, 1.0, 0.0).astype(BF), preferred_element_type=F32
    )
    place_ref[...] = jnp.where(mask > 0, ranks, -1.0).astype(jnp.int32)


def slot_matrix(places):
    ranks = lax.broadcasted_iota(jnp.int32, (CAP, places.shape[1]), 0)
    return jnp.where(ranks == places, 1.0, 0.0)


def gate_up_kernel(steps, spot_ref, *refs):
    token_refs = refs[:8]
    place_ref, gain_ref, keep_ref, first_ref, second_ref = refs[8:13]
    out_refs = refs[13 : 13 + 2 * len(steps)]
    tokens_ref, weight_ref, rows_ref, sems = refs[13 + 2 * len(steps) :]
    tokens = token_refs[0].shape[2]
    columns, width = keep_ref.shape[1:]
    copies = []
    for piece in range(8):
        for jx in range(2):
            copies.append(
                pltpu.make_async_copy(
                    token_refs[piece].at[jx],
                    tokens_ref.at[jx * NY + piece // 2, :, pl.ds(piece % 2 * tokens, tokens)],
                    sems.at[piece * 2 + jx],
                )
            )
    most = first_ref.shape[0]
    mine = pl.multiple_of(spot_ref[1] * columns, columns)
    other = pl.multiple_of((1 - spot_ref[1]) * columns, columns)
    loads = [
        pltpu.make_async_copy(
            keep_ref.at[spot_ref[1]], weight_ref.at[pl.ds(mine, columns)], sems.at[16]
        ),
        pltpu.make_async_copy(first_ref, weight_ref.at[pl.ds(other, most)], sems.at[17]),
        pltpu.make_async_copy(
            second_ref, weight_ref.at[pl.ds(other + most, columns - most)], sems.at[18]
        ),
    ]
    for copy in copies + loads:
        copy.start()
    for copy in copies:
        copy.wait()
    for i, step in enumerate(steps):
        chunk = (spot_ref[0] + step) % NZ
        empty = jnp.zeros((CAP, tokens), F32)
        first = slot_matrix(place_ref[pl.ds(chunk * 2, 1)])
        second = slot_matrix(place_ref[pl.ds(chunk * 2 + 1, 1)])
        picks = jnp.concatenate(
            [
                jnp.concatenate([first, empty], axis=1),
                jnp.concatenate([empty, second], axis=1),
            ],
            axis=0,
        ).astype(BF)
        rows = lax.dot_general(
            picks, tokens_ref[chunk], (((1,), (1,)), ((), ())), preferred_element_type=F32
        )
        squares = jnp.sum(rows * rows, axis=1, keepdims=True)
        squares = jnp.broadcast_to(squares, (2 * CAP, 128)).astype(BF)
        out_refs[2 * i][:, width:] = squares[:CAP]
        out_refs[2 * i + 1][:, width:] = squares[CAP:]
        rows_ref[i] = (rows * gain_ref[...]).astype(BF)
    for load in loads:
        load.wait()
    tile = 1536
    rows = rows_ref[...].reshape(len(steps) * 2 * CAP, 2 * columns)
    for n in range(0, width, tile):
        hidden = jnp.dot(
            rows, weight_ref[:, n : n + tile], preferred_element_type=F32
        ).astype(BF)
        for i in range(2 * len(steps)):
            out_refs[i][:, n : n + tile] = hidden[i * CAP : (i + 1) * CAP]


def down_kernel(steps, spot_ref, *refs):
    count = len(steps)
    act_refs = refs[: 2 * count]
    keep_ref, taken_ref, place_ref, gain_ref, own_ref, other_ref = refs[2 * count : 2 * count + 6]
    acts_ref, outs_ref = refs[2 * count + 6 :]
    spread = 128
    for i, act_ref in enumerate(act_refs):
        first = i // 2 * spread + i % 2 * CAP
        acts_ref[first : first + CAP] = act_ref[...]
    left = spread - 2 * CAP
    for i in range(count):
        acts_ref[i * spread + 2 * CAP : (i + 1) * spread] = jnp.zeros(
            (left, acts_ref.shape[1]), BF
        )
    picks, gains = [], []
    tokens = place_ref.shape[1]
    empty = jnp.zeros((CAP, tokens), F32)
    for i in range(count):
        chunk = (spot_ref[0] + steps[i] + NZ) % NZ
        first = slot_matrix(place_ref[pl.ds(chunk * 2, 1)])
        second = slot_matrix(place_ref[pl.ds(chunk * 2 + 1, 1)])
        pick = [
            jnp.concatenate([first, empty], axis=1),
            jnp.concatenate([empty, second], axis=1),
            jnp.zeros((left, 2 * tokens), F32),
        ]
        picks.append(jnp.concatenate(pick, axis=0).astype(BF))
        gains.append([gain_ref[pl.ds(chunk * 2 + c, 1)] for c in range(2)])
    for half, weight in enumerate((keep_ref[spot_ref[1]], taken_ref[...])):
        outs_ref[half] = lax.dot_general(
            weight, acts_ref[...], (((1,), (1,)), ((), ())), preferred_element_type=F32
        ).astype(BF)
    for i in range(count):
        for half in range(2):
            rows = jnp.dot(
                outs_ref[half, :, i * spread : (i + 1) * spread],
                picks[i],
                preferred_element_type=F32,
            )
            own_ref[half, i] = (rows[:, :tokens] * gains[i][0]).astype(BF)
            other_ref[half, i] = (rows[:, tokens:] * gains[i][1]).astype(BF)


def merge_kernel(groups, z_ref, *refs):
    for g, steps in enumerate(groups):
        own_ref, taken_ref = refs[2 * g : 2 * g + 2]
        for i, step in enumerate(steps):
            chunk = (z_ref[0] + step + NZ) % NZ
            for half in range(2):
                total = plus(own_ref[half, i], taken_ref[half, i])
                for jx in range(2):
                    out_ref = refs[2 * len(groups) + 2 * jx + half]

                    @pl.when(chunk // NY == jx)
                    def _():
                        out_ref[chunk % NY] = total


def body(
    residual,
    query_nope,
    query_rope,
    latent,
    key_rope,
    key_lift,
    value_lift,
    out_weight,
    norm_gain,
    gate_up_weight,
    down_weight,
    route_ids,
    route_weights,
):
    rows, columns = residual.shape
    heads, width, nope = key_lift.shape
    rope = key_rope.shape[1]
    topk = route_ids.shape[1]
    hidden = down_weight.shape[1]
    model_width = out_weight.shape[1]
    score_scale = 1.0 / math.sqrt(nope + rope)
    xh, y, core = lax.axis_index("xh"), lax.axis_index("y"), lax.axis_index("core")
    xl, z = lax.axis_index("xl"), lax.axis_index("z")
    shard = (xh * NY + y) * 2 + core

    with jax.named_scope("gather_keys"):
        packed = vmem_call(
            pack_kernel,
            jax.ShapeDtypeStruct((rows, width + 128), BF),
            [ANY] * 4,
            [
                pltpu.VMEM((rows, width), BF),
                pltpu.VMEM((rope, rows), BF),
                pltpu.VMEM((topk, rows), jnp.int32),
                pltpu.VMEM((topk, rows), F32),
                pltpu.VMEM((128, rows), F32),
                pltpu.SemaphoreType.DMA((4,)),
            ],
            10**6,
            "pack",
            grant=60,
        )(latent, key_rope.T, route_ids.T, route_weights.T)
        along_x = jnp.concatenate([packed, xor_x(packed, 3)], axis=0)
        pieces = []
        for ahead in range(NY):
            pieces.append(along_x if ahead == 0 else from_y(along_x, ahead))

    with jax.named_scope("swap_weights"):
        up = after(gate_up_weight, along_x)
        most = columns * 13 // 20
        up_gives = [
            lax.dynamic_slice(up, (1 - xl, first, 0), (1, last - first, 2 * hidden)).reshape(
                last - first, 2 * hidden
            )
            for first, last in ((0, most), (most, columns))
        ]
        up_takens = [xor_x(give, 1) for give in up_gives]

        def in_order(own, other):
            return jnp.where(
                xl == 0, jnp.concatenate([own, other]), jnp.concatenate([other, own])
            )

        parts, rest = [], norm_gain
        for _ in range(3):
            parts.append(lax.reduce_precision(rest, 8, 7))
            rest = rest - parts[-1]
        parts = jnp.concatenate(parts + [jnp.zeros((8 * rows - 3 * columns,), F32)])
        notes = jnp.concatenate([residual.T, parts.astype(BF).reshape(8, rows)])
        notes = xor_x(notes, 1)
        residual_columns = in_order(residual.T, notes[:columns])
        parts = notes[columns:].astype(F32).reshape(-1)
        gain_other = parts[:columns] + parts[columns : 2 * columns] + parts[2 * columns :][:columns]
        gain_columns = in_order(norm_gain, gain_other)[None, :]

    with jax.named_scope("attention"):
        query_heads = query_nope.reshape(rows, heads, nope)
        query_latent = jnp.einsum(
            "thn,hln->htl", query_heads, key_lift, preferred_element_type=F32
        ).astype(BF)
        query_rotary = jnp.transpose(query_rope.reshape(rows, heads, rope), (1, 0, 2))
        queries = jnp.concatenate(
            [query_latent, query_rotary, jnp.zeros((heads, rows, 128 - rope), BF)], axis=2
        ).reshape(heads * rows, width + 128)
        starts = []
        for ahead in range(NY):
            for flip in range(2):
                for jx in range(2):
                    starts.append(((xh ^ jx) * NY + (y + ahead) % NY) * 2 + (core ^ flip))
        places = jnp.stack(starts)[:, None] * rows + jnp.arange(rows, dtype=jnp.int32)[None, :]
        places = places.reshape(1, -1)
        spot = jnp.stack([shard * rows, z])
        queries = after(queries, *up_gives)
        lines = heads * rows
        early = [pieces[0], swap_core(pieces[0])]
        count = len(early)
        keys = count * 2 * rows

        def state(keys):
            return [pltpu.VMEM((keys, width + 128), BF)]

        def sheets(keys):
            return [pltpu.VMEM((lines, keys), F32), pltpu.VMEM((lines, keys), BF)]

        total, top, mass, early_notes = vmem_call(
            functools.partial(attention_start_kernel, score_scale, count, heads),
            (
                jax.ShapeDtypeStruct((lines, width), F32),
                jax.ShapeDtypeStruct((lines, 128), F32),
                jax.ShapeDtypeStruct((lines, 128), F32),
                jax.ShapeDtypeStruct((count, 2 * rows, 128), BF),
            ),
            [SMEM] + [VMEM] * (2 + count),
            state(keys) + sheets(keys) + [pltpu.SemaphoreType.DMA((count,))],
            3 * 10**9,
            "attention_start",
        )(spot, queries, *early, places[:, :keys])
        late = [after(mine, total) for mine in pieces[1:]]
        late = [piece for mine in late for piece in (mine, swap_core(mine))]
        count = len(late)
        late_keys = count * 2 * rows
        partial_mix, late_notes = vmem_call(
            functools.partial(attention_kernel, score_scale, count),
            (
                jax.ShapeDtypeStruct((NZ, 2 * columns, rows), BF),
                jax.ShapeDtypeStruct((count, 2 * rows, 128), BF),
            ),
            [SMEM] + [VMEM] * (5 + count) + [ANY] * 2,
            state(late_keys)
            + [
                pltpu.VMEM(value_lift.shape, BF),
                pltpu.VMEM(out_weight.shape, BF),
            ]
            + sheets(late_keys)
            + [
                pltpu.VMEM((rows, heads * value_lift.shape[2]), BF),
                pltpu.SemaphoreType.DMA((count + 2,)),
            ],
            10**6,
            "attention",
        )(
            spot,
            queries,
            *late,
            places[:, keys:],
            total,
            top,
            mass,
            value_lift,
            out_weight,
        )

    with jax.named_scope("routing"):
        place, gain = vmem_call(
            functools.partial(routing_kernel, rope),
            (
                jax.ShapeDtypeStruct((2 * NZ, rows), jnp.int32),
                jax.ShapeDtypeStruct((2 * NZ, rows), F32),
            ),
            [SMEM] + [VMEM] * 2,
            [pltpu.VMEM((2 * NZ, rows), F32)],
            10**6,
            "routing",
        )((2 * shard + xl).reshape(1), early_notes, late_notes)

    with jax.named_scope("sum_mix"):
        partial_mix = after(partial_mix, up_takens[0])
        ahead_in, back_in = to_z(partial_mix[4], 1), None
        partial_mix = after(partial_mix, place, gain, gain_columns, residual_columns)
        for step in (3, 2, 1):
            ahead_out, back_out = plus(partial_mix[step], ahead_in), partial_mix[NZ - step]
            if back_in is not None:
                back_out = plus(back_out, back_in)
            ahead_in, back_in = to_z(ahead_out, 1), to_z(back_out, -1)
        mix = partial_mix[0].astype(F32) + ahead_in.astype(F32) + back_in.astype(F32)
        mix = after(mix.astype(BF), up_takens[1])
        mix = mix.astype(F32) + xor_x(mix, 1).astype(F32)
        mixed = (residual_columns.astype(F32) + mix).astype(BF)

    with jax.named_scope("gather_tokens"):
        along_x = jnp.stack([mixed, xor_x(mixed, 3)])
        token_pieces = []
        for ahead in range(NY):
            mine = along_x if ahead == 0 else from_y(along_x, ahead)
            token_pieces += [mine, swap_core(mine)]

    with jax.named_scope("swap_weights"):
        down = after(jnp.swapaxes(down_weight, 1, 2), *token_pieces)
        down_taken = xor_x(lax.dynamic_index_in_dim(down, 1 - xl, 0, keepdims=False), 1)

    with jax.named_scope("gate_up"):
        wide = 2 * hidden + 128
        spot = jnp.stack([z, xl])
        partial_hidden = {}
        for steps in ((4, 3, 5), (6, 2, 7, 1, 0)):
            flat = vmem_call(
                functools.partial(gate_up_kernel, steps),
                (jax.ShapeDtypeStruct((CAP, wide), BF),) * (2 * len(steps)),
                [SMEM] + [ANY] * 8 + [VMEM] * 2 + [ANY] * 3,
                [
                    pltpu.VMEM((NZ, 2 * columns, 2 * rows), BF),
                    pltpu.VMEM((2 * columns, 2 * hidden), BF),
                    pltpu.VMEM((len(steps), 2 * CAP, 2 * columns), BF),
                    pltpu.SemaphoreType.DMA((19,)),
                ],
                4 * 10**9,
                "gate_up",
            )(spot, *token_pieces, place, gain_columns, gate_up_weight, *up_takens)
            partial_hidden.update({k: list(flat[2 * i : 2 * i + 2]) for i, k in enumerate(steps)})

    with jax.named_scope("sum_hidden"):
        ahead_in = [to_z(partial_hidden[4][0], 1), None]
        back_in = [None, to_z(partial_hidden[4][1], -1)]
        for step in (3, 2, 1):
            for c in (1, 0):
                out = partial_hidden[step][c]
                if ahead_in[c] is not None:
                    out = plus(out, ahead_in[c])
                ahead_in[c] = to_z(out, 1)
                out = partial_hidden[NZ - step][1 - c]
                if back_in[1 - c] is not None:
                    out = plus(out, back_in[1 - c])
                back_in[1 - c] = to_z(out, -1)
        acts = []
        for c in range(2):
            full = partial_hidden[0][c].astype(F32) + ahead_in[c].astype(F32)
            full = full + back_in[c].astype(F32)
            factor = lax.rsqrt(full[:, 2 * hidden : 2 * hidden + 1] / model_width + NORM_EPS)
            full = full * factor
            acts.append((jax.nn.silu(full[:, :hidden]) * full[:, hidden : 2 * hidden]).astype(BF))

    with jax.named_scope("gather_hidden"):
        chunks = {0: acts}
        for step in (1, 2, 3):
            chunks[-step] = [to_z(chunks[1 - step][c], 1) for c in range(2)]
            chunks[step] = [to_z(chunks[step - 1][c], -1) for c in range(2)]
        chunks[4] = [to_z(chunks[-3][0], 1), to_z(chunks[3][1], -1)]

    with jax.named_scope("down"):
        groups = ((0, -1, 1, -2, 2), (-3, 3, 4))
        parts = []
        for steps in groups:
            count = len(steps)
            own_rows, other_rows = vmem_call(
                functools.partial(down_kernel, steps),
                (jax.ShapeDtypeStruct((2, count, columns, rows), BF),) * 2,
                [SMEM] + [VMEM] * (2 * count + 4),
                [
                    pltpu.VMEM((count * 128, hidden), BF),
                    pltpu.VMEM((2, columns, count * 128), BF),
                ],
                2 * 10**9,
                "down",
            )(
                spot,
                *[chunks[step][c] for step in steps for c in range(2)],
                down,
                down_taken,
                place,
                gain,
            )
            parts += [own_rows, swap_core(other_rows)]

    with jax.named_scope("return_rows"):
        gives = vmem_call(
            functools.partial(merge_kernel, groups),
            (jax.ShapeDtypeStruct((NY, columns, rows), BF),) * 4,
            [SMEM] + [VMEM] * 4,
            [],
            10**7,
            "merge",
        )(z.reshape(1), *parts)
        total = gives[0].astype(F32)
        for bits in (1, 2, 3):
            total = total + xor_x(gives[bits], bits).astype(F32)
        routed = total[0]
        for ahead in range(1, NY):
            routed = routed + from_y(total[ahead].astype(BF), -ahead).astype(F32)
        mine = lax.dynamic_slice_in_dim(mixed, xl * columns, columns, axis=0)
        return (mine.astype(F32) + routed).astype(BF).T


def solution(mesh):
    fine = Mesh(mesh.devices.reshape(2, NY, 2, 2, NZ), AXES)
    return jax.shard_map(
        body,
        mesh=fine,
        in_specs=(
            P(SEQ, EXP),
            P(SEQ, EXP),
            P(SEQ, EXP),
            P(SEQ, None),
            P(SEQ, None),
            P(EXP, None, None),
            P(EXP, None, None),
            P(EXP, None),
            P(EXP),
            P(SEQ, EXP, None),
            P(SEQ, None, EXP),
            P(SEQ, None),
            P(SEQ, None),
        ),
        out_specs=P(SEQ, EXP),
        check_vma=False,
    )
```

```python
import functools
import math

import jax
import jax.numpy as jnp
from jax import lax
from jax.experimental import pallas as pl
from jax.experimental.pallas import tpu as pltpu
from jax.sharding import Mesh, PartitionSpec as P

CAP = 48
NORM_EPS = 1e-06
BF = jnp.bfloat16
F32 = jnp.float32

AXES = ("xh", "y", "core", "xl", "z")
SEQ = ("xh", "y", "core")
EXP = ("xl", "z")
NX, NY, NZ = 4, 4, 8


def xor_x(value, bits):
    return lax.ppermute(value, ("xh", "xl"), [(s, s ^ bits) for s in range(NX)])


def from_y(value, ahead):
    return lax.ppermute(value, "y", [(s, (s - ahead) % NY) for s in range(NY)])


def swap_core(value):
    return lax.ppermute(value, "core", [(0, 1), (1, 0)])


def to_z(value, ahead):
    return lax.ppermute(value, "z", [(s, (s + ahead) % NZ) for s in range(NZ)])


def after(value, *earlier):
    return lax.optimization_barrier((value, *earlier))[0]


def plus(a, b):
    return (a.astype(F32) + b.astype(F32)).astype(BF)


VMEM = pl.BlockSpec(memory_space=pltpu.VMEM)
SMEM = pl.BlockSpec(memory_space=pltpu.SMEM)
ANY = pl.BlockSpec(memory_space=pl.ANY)


def vmem_call(kernel, out_shape, in_specs, scratch, flops, name, grant=24):
    return pl.pallas_call(
        kernel,
        out_shape=out_shape,
        in_specs=in_specs,
        out_specs=jax.tree.map(lambda _: VMEM, out_shape),
        scratch_shapes=scratch,
        compiler_params=pltpu.CompilerParams(vmem_limit_bytes=grant * 2**20),
        cost_estimate=pl.CostEstimate(flops=flops, bytes_accessed=flops // 256, transcendentals=0),
        name=name,
    )


def load_all(sources, targets, sems):
    copies = [
        pltpu.make_async_copy(source, target, sems.at[i])
        for i, (source, target) in enumerate(zip(sources, targets))
    ]
    for copy in copies:
        copy.start()
    return copies


def pack_kernel(latent_in, rope_in, ids_in, gains_in, out_ref, *scratch):
    latent_ref, rope_ref, ids_ref, gains_ref, notes_ref, sems = scratch
    width, rope, topk = latent_ref.shape[1], rope_ref.shape[0], ids_ref.shape[0]
    copies = load_all(
        (latent_in, rope_in, ids_in, gains_in), (latent_ref, rope_ref, ids_ref, gains_ref), sems
    )
    notes_ref[rope:] = jnp.zeros((notes_ref.shape[0] - rope, notes_ref.shape[1]), F32)
    notes_ref[rope : rope + 8] = jnp.full((8, notes_ref.shape[1]), -1.0, F32)
    for copy in copies:
        copy.wait()
    notes_ref[:rope] = rope_ref[...].astype(F32)
    notes_ref[rope : rope + topk] = ids_ref[...].astype(F32)
    rest = gains_ref[...]
    for part in range(1, 4):
        rounded = rest.astype(BF).astype(F32)
        notes_ref[rope + 8 * part : rope + 8 * part + topk] = rounded
        rest = rest - rounded
    out_ref[:, :width] = latent_ref[...]
    out_ref[:, width:] = jnp.transpose(notes_ref[...]).astype(BF)


def score_pieces(score_scale, heads, spot_ref, q_ref, places_ref, kv_refs, scores_ref, notes_ref):
    rows = q_ref.shape[0] // heads
    keys = kv_refs[0].shape[0]
    width = kv_refs[0].shape[1] - 128
    query_places = spot_ref[0] + lax.broadcasted_iota(jnp.int32, (rows, keys), 0)
    tops = [None] * heads
    for p, kv_ref in enumerate(kv_refs):
        here = slice(p * keys, (p + 1) * keys)
        notes_ref[p] = kv_ref[:, width:]
        allowed = places_ref[:, here] <= query_places
        scores = lax.dot_general(
            q_ref[...], kv_ref[...], (((1,), (1,)), ((), ())), preferred_element_type=F32
        )
        for h in range(heads):
            lines = slice(h * rows, (h + 1) * rows)
            masked = jnp.where(allowed, scores[lines] * score_scale, -1e30)
            scores_ref[lines, here] = masked
            for lane in range(0, keys, 128):
                part = masked[:, lane : lane + 128]
                tops[h] = part if tops[h] is None else jnp.maximum(tops[h], part)
    return [jnp.max(top, axis=1, keepdims=True) for top in tops]


def weigh_pieces(tops, pieces, scores_ref, weights_ref):
    heads = len(tops)
    rows, keys = scores_ref.shape[0] // heads, scores_ref.shape[1] // pieces
    masses = [None] * heads
    for h in range(heads):
        lines = slice(h * rows, (h + 1) * rows)
        for p in range(pieces):
            here = slice(p * keys, (p + 1) * keys)
            weights = jnp.exp(scores_ref[lines, here] - tops[h])
            for lane in range(0, keys, 128):
                part = weights[:, lane : lane + 128]
                masses[h] = part if masses[h] is None else masses[h] + part
            weights_ref[lines, here] = weights.astype(BF)
    return [jnp.sum(mass, axis=1, keepdims=True) for mass in masses]


def attention_start_kernel(score_scale, pieces, heads, spot_ref, q_ref, *refs):
    kv_refs = refs[:pieces]
    places_ref, total_ref, top_ref, mass_ref, notes_ref = refs[pieces : pieces + 5]
    kv_ref, scores_ref, weights_ref, sems = refs[pieces + 5 :]
    keys = kv_refs[0].shape[0]
    copies = load_all(kv_refs, [kv_ref.at[pl.ds(p * keys, keys)] for p in range(pieces)], sems)
    tops = score_pieces(
        score_scale, heads, spot_ref, q_ref, places_ref, kv_refs, scores_ref, notes_ref
    )
    masses = weigh_pieces(tops, pieces, scores_ref, weights_ref)
    for copy in copies:
        copy.wait()
    width = total_ref.shape[1]
    total_ref[...] = jnp.dot(weights_ref[...], kv_ref[:, :width], preferred_element_type=F32)
    rows = q_ref.shape[0] // heads
    for h in range(heads):
        lines = slice(h * rows, (h + 1) * rows)
        top_ref[lines] = jnp.broadcast_to(tops[h], (rows, 128))
        mass_ref[lines] = jnp.broadcast_to(masses[h], (rows, 128))


def attention_kernel(score_scale, pieces, spot_ref, q_ref, *refs):
    kv_refs = refs[:pieces]
    places_ref, before_ref, top_ref, mass_ref, lift_ref, mix_ref, out_ref, notes_ref = refs[
        pieces : pieces + 8
    ]
    kv_ref, scores_ref, weights_ref, values_ref, sems = refs[pieces + 8 :]
    heads, width, value_width = lift_ref.shape
    rows = q_ref.shape[0] // heads
    keys = kv_refs[0].shape[0]
    copies = load_all(kv_refs, [kv_ref.at[pl.ds(p * keys, keys)] for p in range(pieces)], sems)
    tops = score_pieces(
        score_scale, heads, spot_ref, q_ref, places_ref, kv_refs, scores_ref, notes_ref
    )
    shrink = []
    for h in range(heads):
        old = top_ref[h * rows : (h + 1) * rows, :1]
        tops[h] = jnp.maximum(tops[h], old)
        shrink.append(jnp.exp(old - tops[h]))
    masses = weigh_pieces(tops, pieces, scores_ref, weights_ref)
    for copy in copies:
        copy.wait()
    total = jnp.dot(weights_ref[...], kv_ref[:, :width], preferred_element_type=F32)
    for h in range(heads):
        lines = slice(h * rows, (h + 1) * rows)
        mass = masses[h] + mass_ref[lines, :1] * shrink[h]
        attended = ((total[lines] + before_ref[lines] * shrink[h]) / mass).astype(BF)
        values_ref[:, h * value_width : (h + 1) * value_width] = jnp.dot(
            attended, lift_ref[h], preferred_element_type=F32
        ).astype(BF)
    two = out_ref.shape[1]
    column = two // 2
    for i in range(NZ // 2):
        parts = []
        for half in range(2):
            first = (half * NZ // 2 + i) * two
            part = jnp.dot(
                values_ref[...], mix_ref[:, first : first + two], preferred_element_type=F32
            )
            parts.append(jnp.transpose(part).astype(BF))
        for odd in range(2):
            step = (2 * i + odd - spot_ref[1] + NZ) % NZ
            for half in range(2):
                out_ref[step, half * column : (half + 1) * column] = parts[half][
                    odd * column : (odd + 1) * column
                ]


def routing_kernel(first, spot_ref, early_ref, late_ref, place_ref, gain_ref, masks_ref):
    rows = place_ref.shape[1]
    blocks = [early_ref[p] for p in range(early_ref.shape[0])]
    blocks += [late_ref[p] for p in range(late_ref.shape[0])]
    for p, block in enumerate(blocks):
        notes = jnp.transpose(block.astype(F32))[first : first + 32]
        for jx in range(2):
            block = notes[:, jx * rows : (jx + 1) * rows]
            named = block[:8] == spot_ref[0].astype(F32)
            gains = block[8:16] + block[16:24] + block[24:32]
            index = (jx * NY + p // 2) * 2 + p % 2
            masks_ref[index : index + 1] = jnp.max(
                jnp.where(named, 1.0, 0.0), axis=0, keepdims=True
            )
            gain_ref[index : index + 1] = jnp.sum(
                jnp.where(named, gains, 0.0), axis=0, keepdims=True
            )
    earlier = lax.broadcasted_iota(jnp.int32, (rows, rows), 0) < lax.broadcasted_iota(
        jnp.int32, (rows, rows), 1
    )
    mask = masks_ref[...]
    ranks = jnp.dot(
        mask.astype(BF), jnp.where(earlier, 1.0, 0.0).astype(BF), preferred_element_type=F32
    )
    place_ref[...] = jnp.where(mask > 0, ranks, -1.0).astype(jnp.int32)


def slot_matrix(places):
    ranks = lax.broadcasted_iota(jnp.int32, (CAP, places.shape[1]), 0)
    return jnp.where(ranks == places, 1.0, 0.0)


def gate_up_kernel(steps, spot_ref, *refs):
    token_refs = refs[:8]
    place_ref, gain_ref, keep_ref, first_ref, second_ref = refs[8:13]
    out_refs = refs[13 : 13 + 2 * len(steps)]
    tokens_ref, weight_ref, rows_ref, sems = refs[13 + 2 * len(steps) :]
    tokens = token_refs[0].shape[2]
    columns, width = keep_ref.shape[1:]
    copies = []
    for piece in range(8):
        for jx in range(2):
            copies.append(
                pltpu.make_async_copy(
                    token_refs[piece].at[jx],
                    tokens_ref.at[jx * NY + piece // 2, :, pl.ds(piece % 2 * tokens, tokens)],
                    sems.at[piece * 2 + jx],
                )
            )
    most = first_ref.shape[0]
    mine = pl.multiple_of(spot_ref[1] * columns, columns)
    other = pl.multiple_of((1 - spot_ref[1]) * columns, columns)
    loads = [
        pltpu.make_async_copy(
            keep_ref.at[spot_ref[1]], weight_ref.at[pl.ds(mine, columns)], sems.at[16]
        ),
        pltpu.make_async_copy(first_ref, weight_ref.at[pl.ds(other, most)], sems.at[17]),
        pltpu.make_async_copy(
            second_ref, weight_ref.at[pl.ds(other + most, columns - most)], sems.at[18]
        ),
    ]
    for copy in copies + loads:
        copy.start()
    for copy in copies:
        copy.wait()
    for i, step in enumerate(steps):
        chunk = (spot_ref[0] + step) % NZ
        empty = jnp.zeros((CAP, tokens), F32)
        first = slot_matrix(place_ref[pl.ds(chunk * 2, 1)])
        second = slot_matrix(place_ref[pl.ds(chunk * 2 + 1, 1)])
        picks = jnp.concatenate(
            [
                jnp.concatenate([first, empty], axis=1),
                jnp.concatenate([empty, second], axis=1),
            ],
            axis=0,
        ).astype(BF)
        rows = lax.dot_general(
            picks, tokens_ref[chunk], (((1,), (1,)), ((), ())), preferred_element_type=F32
        )
        squares = jnp.sum(rows * rows, axis=1, keepdims=True)
        squares = jnp.broadcast_to(squares, (2 * CAP, 128)).astype(BF)
        out_refs[2 * i][:, width:] = squares[:CAP]
        out_refs[2 * i + 1][:, width:] = squares[CAP:]
        rows_ref[i] = (rows * gain_ref[...]).astype(BF)
    for load in loads:
        load.wait()
    tile = 1536
    rows = rows_ref[...].reshape(len(steps) * 2 * CAP, 2 * columns)
    for n in range(0, width, tile):
        hidden = jnp.dot(
            rows, weight_ref[:, n : n + tile], preferred_element_type=F32
        ).astype(BF)
        for i in range(2 * len(steps)):
            out_refs[i][:, n : n + tile] = hidden[i * CAP : (i + 1) * CAP]


def down_kernel(steps, spot_ref, *refs):
    count = len(steps)
    act_refs = refs[: 2 * count]
    keep_ref, taken_ref, place_ref, gain_ref, own_ref, other_ref = refs[2 * count : 2 * count + 6]
    acts_ref, outs_ref = refs[2 * count + 6 :]
    spread = 128
    for i, act_ref in enumerate(act_refs):
        first = i // 2 * spread + i % 2 * CAP
        acts_ref[first : first + CAP] = act_ref[...]
    left = spread - 2 * CAP
    for i in range(count):
        acts_ref[i * spread + 2 * CAP : (i + 1) * spread] = jnp.zeros(
            (left, acts_ref.shape[1]), BF
        )
    picks, gains = [], []
    tokens = place_ref.shape[1]
    empty = jnp.zeros((CAP, tokens), F32)
    for i in range(count):
        chunk = (spot_ref[0] + steps[i] + NZ) % NZ
        first = slot_matrix(place_ref[pl.ds(chunk * 2, 1)])
        second = slot_matrix(place_ref[pl.ds(chunk * 2 + 1, 1)])
        pick = [
            jnp.concatenate([first, empty], axis=1),
            jnp.concatenate([empty, second], axis=1),
            jnp.zeros((left, 2 * tokens), F32),
        ]
        picks.append(jnp.concatenate(pick, axis=0).astype(BF))
        gains.append([gain_ref[pl.ds(chunk * 2 + c, 1)] for c in range(2)])
    for half, weight in enumerate((keep_ref[spot_ref[1]], taken_ref[...])):
        outs_ref[half] = lax.dot_general(
            weight, acts_ref[...], (((1,), (1,)), ((), ())), preferred_element_type=F32
        ).astype(BF)
    for i in range(count):
        for half in range(2):
            rows = jnp.dot(
                outs_ref[half, :, i * spread : (i + 1) * spread],
                picks[i],
                preferred_element_type=F32,
            )
            own_ref[half, i] = (rows[:, :tokens] * gains[i][0]).astype(BF)
            other_ref[half, i] = (rows[:, tokens:] * gains[i][1]).astype(BF)


def merge_kernel(groups, z_ref, *refs):
    for g, steps in enumerate(groups):
        own_ref, taken_ref = refs[2 * g : 2 * g + 2]
        for i, step in enumerate(steps):
            chunk = (z_ref[0] + step + NZ) % NZ
            for half in range(2):
                total = plus(own_ref[half, i], taken_ref[half, i])
                for jx in range(2):
                    out_ref = refs[2 * len(groups) + 2 * jx + half]

                    @pl.when(chunk // NY == jx)
                    def _():
                        out_ref[chunk % NY] = total


def body(
    residual,
    query_nope,
    query_rope,
    latent,
    key_rope,
    key_lift,
    value_lift,
    out_weight,
    norm_gain,
    gate_up_weight,
    down_weight,
    route_ids,
    route_weights,
):
    rows, columns = residual.shape
    heads, width, nope = key_lift.shape
    rope = key_rope.shape[1]
    topk = route_ids.shape[1]
    hidden = down_weight.shape[1]
    model_width = out_weight.shape[1]
    score_scale = 1.0 / math.sqrt(nope + rope)
    xh, y, core = lax.axis_index("xh"), lax.axis_index("y"), lax.axis_index("core")
    xl, z = lax.axis_index("xl"), lax.axis_index("z")
    shard = (xh * NY + y) * 2 + core

    with jax.named_scope("gather_keys"):
        packed = vmem_call(
            pack_kernel,
            jax.ShapeDtypeStruct((rows, width + 128), BF),
            [ANY] * 4,
            [
                pltpu.VMEM((rows, width), BF),
                pltpu.VMEM((rope, rows), BF),
                pltpu.VMEM((topk, rows), jnp.int32),
                pltpu.VMEM((topk, rows), F32),
                pltpu.VMEM((128, rows), F32),
                pltpu.SemaphoreType.DMA((4,)),
            ],
            10**6,
            "pack",
            grant=60,
        )(latent, key_rope.T, route_ids.T, route_weights.T)
        along_x = jnp.concatenate([packed, xor_x(packed, 3)], axis=0)
        pieces = []
        for ahead in range(NY):
            pieces.append(along_x if ahead == 0 else from_y(along_x, ahead))

    with jax.named_scope("swap_weights"):
        up = after(gate_up_weight, along_x)
        most = columns * 13 // 20
        up_gives = [
            lax.dynamic_slice(up, (1 - xl, first, 0), (1, last - first, 2 * hidden)).reshape(
                last - first, 2 * hidden
            )
            for first, last in ((0, most), (most, columns))
        ]
        up_takens = [xor_x(give, 1) for give in up_gives]

        def in_order(own, other):
            return jnp.where(
                xl == 0, jnp.concatenate([own, other]), jnp.concatenate([other, own])
            )

        parts, rest = [], norm_gain
        for _ in range(3):
            parts.append(lax.reduce_precision(rest, 8, 7))
            rest = rest - parts[-1]
        parts = jnp.concatenate(parts + [jnp.zeros((8 * rows - 3 * columns,), F32)])
        notes = jnp.concatenate([residual.T, parts.astype(BF).reshape(8, rows)])
        notes = xor_x(notes, 1)
        residual_columns = in_order(residual.T, notes[:columns])
        parts = notes[columns:].astype(F32).reshape(-1)
        gain_other = parts[:columns] + parts[columns : 2 * columns] + parts[2 * columns :][:columns]
        gain_columns = in_order(norm_gain, gain_other)[None, :]

    with jax.named_scope("attention"):
        query_heads = query_nope.reshape(rows, heads, nope)
        query_latent = jnp.einsum(
            "thn,hln->htl", query_heads, key_lift, preferred_element_type=F32
        ).astype(BF)
        query_rotary = jnp.transpose(query_rope.reshape(rows, heads, rope), (1, 0, 2))
        queries = jnp.concatenate(
            [query_latent, query_rotary, jnp.zeros((heads, rows, 128 - rope), BF)], axis=2
        ).reshape(heads * rows, width + 128)
        starts = []
        for ahead in range(NY):
            for flip in range(2):
                for jx in range(2):
                    starts.append(((xh ^ jx) * NY + (y + ahead) % NY) * 2 + (core ^ flip))
        places = jnp.stack(starts)[:, None] * rows + jnp.arange(rows, dtype=jnp.int32)[None, :]
        places = places.reshape(1, -1)
        spot = jnp.stack([shard * rows, z])
        queries = after(queries, *up_gives)
        lines = heads * rows
        early = [pieces[0], swap_core(pieces[0])]
        count = len(early)
        keys = count * 2 * rows

        def state(keys):
            return [pltpu.VMEM((keys, width + 128), BF)]

        def sheets(keys):
            return [pltpu.VMEM((lines, keys), F32), pltpu.VMEM((lines, keys), BF)]

        total, top, mass, early_notes = vmem_call(
            functools.partial(attention_start_kernel, score_scale, count, heads),
            (
                jax.ShapeDtypeStruct((lines, width), F32),
                jax.ShapeDtypeStruct((lines, 128), F32),
                jax.ShapeDtypeStruct((lines, 128), F32),
                jax.ShapeDtypeStruct((count, 2 * rows, 128), BF),
            ),
            [SMEM] + [VMEM] * (2 + count),
            state(keys) + sheets(keys) + [pltpu.SemaphoreType.DMA((count,))],
            3 * 10**9,
            "attention_start",
        )(spot, queries, *early, places[:, :keys])
        late = [after(mine, total) for mine in pieces[1:]]
        late = [piece for mine in late for piece in (mine, swap_core(mine))]
        count = len(late)
        late_keys = count * 2 * rows
        partial_mix, late_notes = vmem_call(
            functools.partial(attention_kernel, score_scale, count),
            (
                jax.ShapeDtypeStruct((NZ, 2 * columns, rows), BF),
                jax.ShapeDtypeStruct((count, 2 * rows, 128), BF),
            ),
            [SMEM] + [VMEM] * (7 + count),
            state(late_keys)
            + sheets(late_keys)
            + [
                pltpu.VMEM((rows, heads * value_lift.shape[2]), BF),
                pltpu.SemaphoreType.DMA((count,)),
            ],
            10**6,
            "attention",
        )(
            spot,
            queries,
            *late,
            places[:, keys:],
            total,
            top,
            mass,
            value_lift,
            out_weight,
        )

    with jax.named_scope("routing"):
        place, gain = vmem_call(
            functools.partial(routing_kernel, rope),
            (
                jax.ShapeDtypeStruct((2 * NZ, rows), jnp.int32),
                jax.ShapeDtypeStruct((2 * NZ, rows), F32),
            ),
            [SMEM] + [VMEM] * 2,
            [pltpu.VMEM((2 * NZ, rows), F32)],
            10**6,
            "routing",
        )((2 * shard + xl).reshape(1), early_notes, late_notes)

    with jax.named_scope("sum_mix"):
        partial_mix = after(partial_mix, up_takens[0])
        ahead_in, back_in = to_z(partial_mix[4], 1), None
        partial_mix = after(partial_mix, place, gain, gain_columns, residual_columns)
        for step in (3, 2, 1):
            ahead_out, back_out = plus(partial_mix[step], ahead_in), partial_mix[NZ - step]
            if back_in is not None:
                back_out = plus(back_out, back_in)
            ahead_in, back_in = to_z(ahead_out, 1), to_z(back_out, -1)
        mix = partial_mix[0].astype(F32) + ahead_in.astype(F32) + back_in.astype(F32)
        mix = after(mix.astype(BF), up_takens[1])
        mix = mix.astype(F32) + xor_x(mix, 1).astype(F32)
        mixed = (residual_columns.astype(F32) + mix).astype(BF)

    with jax.named_scope("gather_tokens"):
        along_x = jnp.stack([mixed, xor_x(mixed, 3)])
        token_pieces = []
        for ahead in range(NY):
            mine = along_x if ahead == 0 else from_y(along_x, ahead)
            token_pieces += [mine, swap_core(mine)]

    with jax.named_scope("swap_weights"):
        down = after(jnp.swapaxes(down_weight, 1, 2), *token_pieces)
        down_taken = xor_x(lax.dynamic_index_in_dim(down, 1 - xl, 0, keepdims=False), 1)

    with jax.named_scope("gate_up"):
        wide = 2 * hidden + 128
        spot = jnp.stack([z, xl])
        partial_hidden = {}
        for steps in ((4, 3, 5), (6, 2, 7, 1, 0)):
            flat = vmem_call(
                functools.partial(gate_up_kernel, steps),
                (jax.ShapeDtypeStruct((CAP, wide), BF),) * (2 * len(steps)),
                [SMEM] + [ANY] * 8 + [VMEM] * 2 + [ANY] * 3,
                [
                    pltpu.VMEM((NZ, 2 * columns, 2 * rows), BF),
                    pltpu.VMEM((2 * columns, 2 * hidden), BF),
                    pltpu.VMEM((len(steps), 2 * CAP, 2 * columns), BF),
                    pltpu.SemaphoreType.DMA((19,)),
                ],
                4 * 10**9,
                "gate_up",
            )(spot, *token_pieces, place, gain_columns, gate_up_weight, *up_takens)
            partial_hidden.update({k: list(flat[2 * i : 2 * i + 2]) for i, k in enumerate(steps)})

    with jax.named_scope("sum_hidden"):
        ahead_in = [to_z(partial_hidden[4][0], 1), None]
        back_in = [None, to_z(partial_hidden[4][1], -1)]
        for step in (3, 2, 1):
            for c in (1, 0):
                out = partial_hidden[step][c]
                if ahead_in[c] is not None:
                    out = plus(out, ahead_in[c])
                ahead_in[c] = to_z(out, 1)
                out = partial_hidden[NZ - step][1 - c]
                if back_in[1 - c] is not None:
                    out = plus(out, back_in[1 - c])
                back_in[1 - c] = to_z(out, -1)
        acts = []
        for c in range(2):
            full = partial_hidden[0][c].astype(F32) + ahead_in[c].astype(F32)
            full = full + back_in[c].astype(F32)
            factor = lax.rsqrt(full[:, 2 * hidden : 2 * hidden + 1] / model_width + NORM_EPS)
            full = full * factor
            acts.append((jax.nn.silu(full[:, :hidden]) * full[:, hidden : 2 * hidden]).astype(BF))

    with jax.named_scope("gather_hidden"):
        chunks = {0: acts}
        for step in (1, 2, 3):
            chunks[-step] = [to_z(chunks[1 - step][c], 1) for c in range(2)]
            chunks[step] = [to_z(chunks[step - 1][c], -1) for c in range(2)]
        chunks[4] = [to_z(chunks[-3][0], 1), to_z(chunks[3][1], -1)]

    with jax.named_scope("down"):
        groups = ((0, -1, 1, -2, 2), (-3, 3, 4))
        parts = []
        for steps in groups:
            count = len(steps)
            own_rows, other_rows = vmem_call(
                functools.partial(down_kernel, steps),
                (jax.ShapeDtypeStruct((2, count, columns, rows), BF),) * 2,
                [SMEM] + [VMEM] * (2 * count + 4),
                [
                    pltpu.VMEM((count * 128, hidden), BF),
                    pltpu.VMEM((2, columns, count * 128), BF),
                ],
                2 * 10**9,
                "down",
            )(
                spot,
                *[chunks[step][c] for step in steps for c in range(2)],
                down,
                down_taken,
                place,
                gain,
            )
            parts += [own_rows, swap_core(other_rows)]

    with jax.named_scope("return_rows"):
        gives = vmem_call(
            functools.partial(merge_kernel, groups),
            (jax.ShapeDtypeStruct((NY, columns, rows), BF),) * 4,
            [SMEM] + [VMEM] * 4,
            [],
            10**7,
            "merge",
        )(z.reshape(1), *parts)
        total = gives[0].astype(F32)
        for bits in (1, 2, 3):
            total = total + xor_x(gives[bits], bits).astype(F32)
        routed = total[0]
        for ahead in range(1, NY):
            routed = routed + from_y(total[ahead].astype(BF), -ahead).astype(F32)
        mine = lax.dynamic_slice_in_dim(mixed, xl * columns, columns, axis=0)
        return (mine.astype(F32) + routed).astype(BF).T


def solution(mesh):
    fine = Mesh(mesh.devices.reshape(2, NY, 2, 2, NZ), AXES)
    return jax.shard_map(
        body,
        mesh=fine,
        in_specs=(
            P(SEQ, EXP),
            P(SEQ, EXP),
            P(SEQ, EXP),
            P(SEQ, None),
            P(SEQ, None),
            P(EXP, None, None),
            P(EXP, None, None),
            P(EXP, None),
            P(EXP),
            P(SEQ, EXP, None),
            P(SEQ, None, EXP),
            P(SEQ, None),
            P(SEQ, None),
        ),
        out_specs=P(SEQ, EXP),
        check_vma=False,
    )
```

```python
import functools
import math

import jax
import jax.numpy as jnp
from jax import lax
from jax.experimental import pallas as pl
from jax.experimental.pallas import tpu as pltpu
from jax.sharding import Mesh, PartitionSpec as P

CAP = 48
NORM_EPS = 1e-06
BF = jnp.bfloat16
F32 = jnp.float32

AXES = ("xh", "y", "core", "xl", "z")
SEQ = ("xh", "y", "core")
EXP = ("xl", "z")
NX, NY, NZ = 4, 4, 8


def xor_x(value, bits):
    return lax.ppermute(value, ("xh", "xl"), [(s, s ^ bits) for s in range(NX)])


def from_y(value, ahead):
    return lax.ppermute(value, "y", [(s, (s - ahead) % NY) for s in range(NY)])


def swap_core(value):
    return lax.ppermute(value, "core", [(0, 1), (1, 0)])


def to_z(value, ahead):
    return lax.ppermute(value, "z", [(s, (s + ahead) % NZ) for s in range(NZ)])


def after(value, *earlier):
    return lax.optimization_barrier((value, *earlier))[0]


def plus(a, b):
    return (a.astype(F32) + b.astype(F32)).astype(BF)


VMEM = pl.BlockSpec(memory_space=pltpu.VMEM)
SMEM = pl.BlockSpec(memory_space=pltpu.SMEM)
ANY = pl.BlockSpec(memory_space=pl.ANY)


def vmem_call(kernel, out_shape, in_specs, scratch, flops, name, grant=24):
    return pl.pallas_call(
        kernel,
        out_shape=out_shape,
        in_specs=in_specs,
        out_specs=jax.tree.map(lambda _: VMEM, out_shape),
        scratch_shapes=scratch,
        compiler_params=pltpu.CompilerParams(vmem_limit_bytes=grant * 2**20),
        cost_estimate=pl.CostEstimate(flops=flops, bytes_accessed=flops // 256, transcendentals=0),
        name=name,
    )


def load_all(sources, targets, sems):
    copies = [
        pltpu.make_async_copy(source, target, sems.at[i])
        for i, (source, target) in enumerate(zip(sources, targets))
    ]
    for copy in copies:
        copy.start()
    return copies


def pack_kernel(latent_in, rope_in, ids_in, gains_in, out_ref, *scratch):
    latent_ref, rope_ref, ids_ref, gains_ref, notes_ref, sems = scratch
    width, rope, topk = latent_ref.shape[1], rope_ref.shape[0], ids_ref.shape[0]
    copies = load_all(
        (latent_in, rope_in, ids_in, gains_in), (latent_ref, rope_ref, ids_ref, gains_ref), sems
    )
    notes_ref[rope:] = jnp.zeros((notes_ref.shape[0] - rope, notes_ref.shape[1]), F32)
    notes_ref[rope : rope + 8] = jnp.full((8, notes_ref.shape[1]), -1.0, F32)
    for copy in copies:
        copy.wait()
    notes_ref[:rope] = rope_ref[...].astype(F32)
    notes_ref[rope : rope + topk] = ids_ref[...].astype(F32)
    rest = gains_ref[...]
    for part in range(1, 4):
        rounded = rest.astype(BF).astype(F32)
        notes_ref[rope + 8 * part : rope + 8 * part + topk] = rounded
        rest = rest - rounded
    out_ref[:, :width] = latent_ref[...]
    out_ref[:, width:] = jnp.transpose(notes_ref[...]).astype(BF)


def score_pieces(score_scale, heads, spot_ref, q_ref, places_ref, kv_refs, scores_ref, notes_ref):
    rows = q_ref.shape[0] // heads
    keys = kv_refs[0].shape[0]
    width = kv_refs[0].shape[1] - 128
    query_places = spot_ref[0] + lax.broadcasted_iota(jnp.int32, (rows, keys), 0)
    tops = [None] * heads
    for p, kv_ref in enumerate(kv_refs):
        here = slice(p * keys, (p + 1) * keys)
        notes_ref[p] = kv_ref[:, width:]
        allowed = places_ref[:, here] <= query_places
        scores = lax.dot_general(
            q_ref[...], kv_ref[...], (((1,), (1,)), ((), ())), preferred_element_type=F32
        )
        for h in range(heads):
            lines = slice(h * rows, (h + 1) * rows)
            masked = jnp.where(allowed, scores[lines] * score_scale, -1e30)
            scores_ref[lines, here] = masked
            for lane in range(0, keys, 128):
                part = masked[:, lane : lane + 128]
                tops[h] = part if tops[h] is None else jnp.maximum(tops[h], part)
    return [jnp.max(top, axis=1, keepdims=True) for top in tops]


def weigh_pieces(tops, pieces, scores_ref, weights_ref):
    heads = len(tops)
    rows, keys = scores_ref.shape[0] // heads, scores_ref.shape[1] // pieces
    masses = [None] * heads
    for h in range(heads):
        lines = slice(h * rows, (h + 1) * rows)
        for p in range(pieces):
            here = slice(p * keys, (p + 1) * keys)
            weights = jnp.exp(scores_ref[lines, here] - tops[h])
            for lane in range(0, keys, 128):
                part = weights[:, lane : lane + 128]
                masses[h] = part if masses[h] is None else masses[h] + part
            weights_ref[lines, here] = weights.astype(BF)
    return [jnp.sum(mass, axis=1, keepdims=True) for mass in masses]


def attention_start_kernel(score_scale, pieces, heads, spot_ref, q_ref, *refs):
    kv_refs = refs[:pieces]
    places_ref, total_ref, top_ref, mass_ref, notes_ref = refs[pieces : pieces + 5]
    kv_ref, scores_ref, weights_ref, sems = refs[pieces + 5 :]
    keys = kv_refs[0].shape[0]
    copies = load_all(kv_refs, [kv_ref.at[pl.ds(p * keys, keys)] for p in range(pieces)], sems)
    tops = score_pieces(
        score_scale, heads, spot_ref, q_ref, places_ref, kv_refs, scores_ref, notes_ref
    )
    masses = weigh_pieces(tops, pieces, scores_ref, weights_ref)
    for copy in copies:
        copy.wait()
    width = total_ref.shape[1]
    total_ref[...] = jnp.dot(weights_ref[...], kv_ref[:, :width], preferred_element_type=F32)
    rows = q_ref.shape[0] // heads
    for h in range(heads):
        lines = slice(h * rows, (h + 1) * rows)
        top_ref[lines] = jnp.broadcast_to(tops[h], (rows, 128))
        mass_ref[lines] = jnp.broadcast_to(masses[h], (rows, 128))


def attention_kernel(score_scale, pieces, spot_ref, q_ref, *refs):
    kv_refs = refs[:pieces]
    places_ref, before_ref, top_ref, mass_ref, lift_ref, mix_ref, out_ref, notes_ref = refs[
        pieces : pieces + 8
    ]
    kv_ref, scores_ref, weights_ref, values_ref, sems = refs[pieces + 8 :]
    heads, width, value_width = lift_ref.shape
    rows = q_ref.shape[0] // heads
    keys = kv_refs[0].shape[0]
    copies = load_all(kv_refs, [kv_ref.at[pl.ds(p * keys, keys)] for p in range(pieces)], sems)
    tops = score_pieces(
        score_scale, heads, spot_ref, q_ref, places_ref, kv_refs, scores_ref, notes_ref
    )
    shrink = []
    for h in range(heads):
        old = top_ref[h * rows : (h + 1) * rows, :1]
        tops[h] = jnp.maximum(tops[h], old)
        shrink.append(jnp.exp(old - tops[h]))
    masses = weigh_pieces(tops, pieces, scores_ref, weights_ref)
    for copy in copies:
        copy.wait()
    total = jnp.dot(weights_ref[...], kv_ref[:, :width], preferred_element_type=F32)
    for h in range(heads):
        lines = slice(h * rows, (h + 1) * rows)
        mass = masses[h] + mass_ref[lines, :1] * shrink[h]
        attended = ((total[lines] + before_ref[lines] * shrink[h]) / mass).astype(BF)
        values_ref[:, h * value_width : (h + 1) * value_width] = jnp.dot(
            attended, lift_ref[h], preferred_element_type=F32
        ).astype(BF)
    two = out_ref.shape[1]
    column = two // 2
    for i in range(NZ // 2):
        parts = []
        for half in range(2):
            first = (half * NZ // 2 + i) * two
            part = jnp.dot(
                values_ref[...], mix_ref[:, first : first + two], preferred_element_type=F32
            )
            parts.append(jnp.transpose(part).astype(BF))
        for odd in range(2):
            step = (2 * i + odd - spot_ref[1] + NZ) % NZ
            for half in range(2):
                out_ref[step, half * column : (half + 1) * column] = parts[half][
                    odd * column : (odd + 1) * column
                ]


def routing_kernel(first, spot_ref, early_ref, late_ref, place_ref, gain_ref, masks_ref):
    rows = place_ref.shape[1]
    blocks = [early_ref[p] for p in range(early_ref.shape[0])]
    blocks += [late_ref[p] for p in range(late_ref.shape[0])]
    for p, block in enumerate(blocks):
        notes = jnp.transpose(block.astype(F32))[first : first + 32]
        for jx in range(2):
            block = notes[:, jx * rows : (jx + 1) * rows]
            named = block[:8] == spot_ref[0].astype(F32)
            gains = block[8:16] + block[16:24] + block[24:32]
            index = (jx * NY + p // 2) * 2 + p % 2
            masks_ref[index : index + 1] = jnp.max(
                jnp.where(named, 1.0, 0.0), axis=0, keepdims=True
            )
            gain_ref[index : index + 1] = jnp.sum(
                jnp.where(named, gains, 0.0), axis=0, keepdims=True
            )
    earlier = lax.broadcasted_iota(jnp.int32, (rows, rows), 0) < lax.broadcasted_iota(
        jnp.int32, (rows, rows), 1
    )
    mask = masks_ref[...]
    ranks = jnp.dot(
        mask.astype(BF), jnp.where(earlier, 1.0, 0.0).astype(BF), preferred_element_type=F32
    )
    place_ref[...] = jnp.where(mask > 0, ranks, -1.0).astype(jnp.int32)


def slot_matrix(places):
    ranks = lax.broadcasted_iota(jnp.int32, (CAP, places.shape[1]), 0)
    return jnp.where(ranks == places, 1.0, 0.0)


def gate_up_kernel(steps, spot_ref, *refs):
    token_refs = refs[:8]
    place_ref, gain_ref, keep_ref, first_ref, second_ref = refs[8:13]
    out_refs = refs[13 : 13 + 2 * len(steps)]
    tokens_ref, weight_ref, rows_ref, sems = refs[13 + 2 * len(steps) :]
    tokens = token_refs[0].shape[2]
    columns, width = keep_ref.shape[1:]
    copies = []
    for piece in range(8):
        for jx in range(2):
            copies.append(
                pltpu.make_async_copy(
                    token_refs[piece].at[jx],
                    tokens_ref.at[jx * NY + piece // 2, :, pl.ds(piece % 2 * tokens, tokens)],
                    sems.at[piece * 2 + jx],
                )
            )
    most = first_ref.shape[0]
    mine = pl.multiple_of(spot_ref[1] * columns, columns)
    other = pl.multiple_of((1 - spot_ref[1]) * columns, columns)
    loads = [
        pltpu.make_async_copy(
            keep_ref.at[spot_ref[1]], weight_ref.at[pl.ds(mine, columns)], sems.at[16]
        ),
        pltpu.make_async_copy(first_ref, weight_ref.at[pl.ds(other, most)], sems.at[17]),
        pltpu.make_async_copy(
            second_ref, weight_ref.at[pl.ds(other + most, columns - most)], sems.at[18]
        ),
    ]
    for copy in copies + loads:
        copy.start()
    for copy in copies:
        copy.wait()
    for i, step in enumerate(steps):
        chunk = (spot_ref[0] + step) % NZ
        empty = jnp.zeros((CAP, tokens), F32)
        first = slot_matrix(place_ref[pl.ds(chunk * 2, 1)])
        second = slot_matrix(place_ref[pl.ds(chunk * 2 + 1, 1)])
        picks = jnp.concatenate(
            [
                jnp.concatenate([first, empty], axis=1),
                jnp.concatenate([empty, second], axis=1),
            ],
            axis=0,
        ).astype(BF)
        rows = lax.dot_general(
            picks, tokens_ref[chunk], (((1,), (1,)), ((), ())), preferred_element_type=F32
        )
        squares = jnp.sum(rows * rows, axis=1, keepdims=True)
        squares = jnp.broadcast_to(squares, (2 * CAP, 128)).astype(BF)
        out_refs[2 * i][:, width:] = squares[:CAP]
        out_refs[2 * i + 1][:, width:] = squares[CAP:]
        rows_ref[i] = (rows * gain_ref[...]).astype(BF)
    for load in loads:
        load.wait()
    tile = 1536
    rows = rows_ref[...].reshape(len(steps) * 2 * CAP, 2 * columns)
    for n in range(0, width, tile):
        hidden = jnp.dot(
            rows, weight_ref[:, n : n + tile], preferred_element_type=F32
        ).astype(BF)
        for i in range(2 * len(steps)):
            out_refs[i][:, n : n + tile] = hidden[i * CAP : (i + 1) * CAP]


def down_kernel(steps, spot_ref, *refs):
    count = len(steps)
    act_refs = refs[: 2 * count]
    keep_ref, taken_ref, place_ref, gain_ref, own_ref, other_ref = refs[2 * count : 2 * count + 6]
    acts_ref, outs_ref = refs[2 * count + 6 :]
    spread = 128
    for i, act_ref in enumerate(act_refs):
        first = i // 2 * spread + i % 2 * CAP
        acts_ref[first : first + CAP] = act_ref[...]
    left = spread - 2 * CAP
    for i in range(count):
        acts_ref[i * spread + 2 * CAP : (i + 1) * spread] = jnp.zeros(
            (left, acts_ref.shape[1]), BF
        )
    picks, gains = [], []
    tokens = place_ref.shape[1]
    empty = jnp.zeros((CAP, tokens), F32)
    for i in range(count):
        chunk = (spot_ref[0] + steps[i] + NZ) % NZ
        first = slot_matrix(place_ref[pl.ds(chunk * 2, 1)])
        second = slot_matrix(place_ref[pl.ds(chunk * 2 + 1, 1)])
        pick = [
            jnp.concatenate([first, empty], axis=1),
            jnp.concatenate([empty, second], axis=1),
            jnp.zeros((left, 2 * tokens), F32),
        ]
        picks.append(jnp.concatenate(pick, axis=0).astype(BF))
        gains.append([gain_ref[pl.ds(chunk * 2 + c, 1)] for c in range(2)])
    for half, weight in enumerate((keep_ref[spot_ref[1]], taken_ref[...])):
        outs_ref[half] = lax.dot_general(
            weight, acts_ref[...], (((1,), (1,)), ((), ())), preferred_element_type=F32
        ).astype(BF)
    for i in range(count):
        for half in range(2):
            rows = jnp.dot(
                outs_ref[half, :, i * spread : (i + 1) * spread],
                picks[i],
                preferred_element_type=F32,
            )
            own_ref[half, i] = (rows[:, :tokens] * gains[i][0]).astype(BF)
            other_ref[half, i] = (rows[:, tokens:] * gains[i][1]).astype(BF)


def merge_kernel(groups, z_ref, *refs):
    for g, steps in enumerate(groups):
        own_ref, taken_ref = refs[2 * g : 2 * g + 2]
        for i, step in enumerate(steps):
            chunk = (z_ref[0] + step + NZ) % NZ
            for half in range(2):
                total = plus(own_ref[half, i], taken_ref[half, i])
                for jx in range(2):
                    out_ref = refs[2 * len(groups) + 2 * jx + half]

                    @pl.when(chunk // NY == jx)
                    def _():
                        out_ref[chunk % NY] = total


def body(
    residual,
    query_nope,
    query_rope,
    latent,
    key_rope,
    key_lift,
    value_lift,
    out_weight,
    norm_gain,
    gate_up_weight,
    down_weight,
    route_ids,
    route_weights,
):
    rows, columns = residual.shape
    heads, width, nope = key_lift.shape
    rope = key_rope.shape[1]
    topk = route_ids.shape[1]
    hidden = down_weight.shape[1]
    model_width = out_weight.shape[1]
    score_scale = 1.0 / math.sqrt(nope + rope)
    xh, y, core = lax.axis_index("xh"), lax.axis_index("y"), lax.axis_index("core")
    xl, z = lax.axis_index("xl"), lax.axis_index("z")
    shard = (xh * NY + y) * 2 + core

    with jax.named_scope("gather_keys"):
        packed = vmem_call(
            pack_kernel,
            jax.ShapeDtypeStruct((rows, width + 128), BF),
            [ANY] * 4,
            [
                pltpu.VMEM((rows, width), BF),
                pltpu.VMEM((rope, rows), BF),
                pltpu.VMEM((topk, rows), jnp.int32),
                pltpu.VMEM((topk, rows), F32),
                pltpu.VMEM((128, rows), F32),
                pltpu.SemaphoreType.DMA((4,)),
            ],
            10**6,
            "pack",
            grant=60,
        )(latent, key_rope.T, route_ids.T, route_weights.T)
        along_x = jnp.concatenate([packed, xor_x(packed, 3)], axis=0)
        pieces = []
        for ahead in range(NY):
            pieces.append(along_x if ahead == 0 else from_y(along_x, ahead))

    with jax.named_scope("swap_weights"):
        up = after(gate_up_weight, along_x)
        most = columns * 7 // 10
        up_gives = [
            lax.dynamic_slice(up, (1 - xl, first, 0), (1, last - first, 2 * hidden)).reshape(
                last - first, 2 * hidden
            )
            for first, last in ((0, most), (most, columns))
        ]
        up_takens = [xor_x(give, 1) for give in up_gives]

        def in_order(own, other):
            return jnp.where(
                xl == 0, jnp.concatenate([own, other]), jnp.concatenate([other, own])
            )

        parts, rest = [], norm_gain
        for _ in range(3):
            parts.append(lax.reduce_precision(rest, 8, 7))
            rest = rest - parts[-1]
        parts = jnp.concatenate(parts + [jnp.zeros((8 * rows - 3 * columns,), F32)])
        notes = jnp.concatenate([residual.T, parts.astype(BF).reshape(8, rows)])
        notes = xor_x(notes, 1)
        residual_columns = in_order(residual.T, notes[:columns])
        parts = notes[columns:].astype(F32).reshape(-1)
        gain_other = parts[:columns] + parts[columns : 2 * columns] + parts[2 * columns :][:columns]
        gain_columns = in_order(norm_gain, gain_other)[None, :]

    with jax.named_scope("attention"):
        query_heads = query_nope.reshape(rows, heads, nope)
        query_latent = jnp.einsum(
            "thn,hln->htl", query_heads, key_lift, preferred_element_type=F32
        ).astype(BF)
        query_rotary = jnp.transpose(query_rope.reshape(rows, heads, rope), (1, 0, 2))
        queries = jnp.concatenate(
            [query_latent, query_rotary, jnp.zeros((heads, rows, 128 - rope), BF)], axis=2
        ).reshape(heads * rows, width + 128)
        starts = []
        for ahead in range(NY):
            for flip in range(2):
                for jx in range(2):
                    starts.append(((xh ^ jx) * NY + (y + ahead) % NY) * 2 + (core ^ flip))
        places = jnp.stack(starts)[:, None] * rows + jnp.arange(rows, dtype=jnp.int32)[None, :]
        places = places.reshape(1, -1)
        spot = jnp.stack([shard * rows, z])
        queries = after(queries, *up_gives)
        lines = heads * rows
        early = [pieces[0], swap_core(pieces[0])]
        count = len(early)
        keys = count * 2 * rows

        def state(keys):
            return [pltpu.VMEM((keys, width + 128), BF)]

        def sheets(keys):
            return [pltpu.VMEM((lines, keys), F32), pltpu.VMEM((lines, keys), BF)]

        total, top, mass, early_notes = vmem_call(
            functools.partial(attention_start_kernel, score_scale, count, heads),
            (
                jax.ShapeDtypeStruct((lines, width), F32),
                jax.ShapeDtypeStruct((lines, 128), F32),
                jax.ShapeDtypeStruct((lines, 128), F32),
                jax.ShapeDtypeStruct((count, 2 * rows, 128), BF),
            ),
            [SMEM] + [VMEM] * (2 + count),
            state(keys) + sheets(keys) + [pltpu.SemaphoreType.DMA((count,))],
            3 * 10**9,
            "attention_start",
        )(spot, queries, *early, places[:, :keys])
        late = [after(mine, total) for mine in pieces[1:]]
        late = [piece for mine in late for piece in (mine, swap_core(mine))]
        count = len(late)
        late_keys = count * 2 * rows
        partial_mix, late_notes = vmem_call(
            functools.partial(attention_kernel, score_scale, count),
            (
                jax.ShapeDtypeStruct((NZ, 2 * columns, rows), BF),
                jax.ShapeDtypeStruct((count, 2 * rows, 128), BF),
            ),
            [SMEM] + [VMEM] * (7 + count),
            state(late_keys)
            + sheets(late_keys)
            + [
                pltpu.VMEM((rows, heads * value_lift.shape[2]), BF),
                pltpu.SemaphoreType.DMA((count,)),
            ],
            10**6,
            "attention",
        )(
            spot,
            queries,
            *late,
            places[:, keys:],
            total,
            top,
            mass,
            value_lift,
            out_weight,
        )

    with jax.named_scope("routing"):
        place, gain = vmem_call(
            functools.partial(routing_kernel, rope),
            (
                jax.ShapeDtypeStruct((2 * NZ, rows), jnp.int32),
                jax.ShapeDtypeStruct((2 * NZ, rows), F32),
            ),
            [SMEM] + [VMEM] * 2,
            [pltpu.VMEM((2 * NZ, rows), F32)],
            10**6,
            "routing",
        )((2 * shard + xl).reshape(1), early_notes, late_notes)

    with jax.named_scope("sum_mix"):
        partial_mix = after(partial_mix, up_takens[0])
        ahead_in, back_in = to_z(partial_mix[4], 1), None
        partial_mix = after(partial_mix, place, gain, gain_columns, residual_columns)
        for step in (3, 2, 1):
            ahead_out, back_out = plus(partial_mix[step], ahead_in), partial_mix[NZ - step]
            if back_in is not None:
                back_out = plus(back_out, back_in)
            ahead_in, back_in = to_z(ahead_out, 1), to_z(back_out, -1)
        mix = partial_mix[0].astype(F32) + ahead_in.astype(F32) + back_in.astype(F32)
        mix = after(mix.astype(BF), up_takens[1])
        mix = mix.astype(F32) + xor_x(mix, 1).astype(F32)
        mixed = (residual_columns.astype(F32) + mix).astype(BF)

    with jax.named_scope("gather_tokens"):
        along_x = jnp.stack([mixed, xor_x(mixed, 3)])
        token_pieces = []
        for ahead in range(NY):
            mine = along_x if ahead == 0 else from_y(along_x, ahead)
            token_pieces += [mine, swap_core(mine)]

    with jax.named_scope("swap_weights"):
        down = after(jnp.swapaxes(down_weight, 1, 2), *token_pieces)
        down_taken = xor_x(lax.dynamic_index_in_dim(down, 1 - xl, 0, keepdims=False), 1)

    with jax.named_scope("gate_up"):
        wide = 2 * hidden + 128
        spot = jnp.stack([z, xl])
        partial_hidden = {}
        for steps in ((4, 3, 5), (6, 2, 7, 1, 0)):
            flat = vmem_call(
                functools.partial(gate_up_kernel, steps),
                (jax.ShapeDtypeStruct((CAP, wide), BF),) * (2 * len(steps)),
                [SMEM] + [ANY] * 8 + [VMEM] * 2 + [ANY] * 3,
                [
                    pltpu.VMEM((NZ, 2 * columns, 2 * rows), BF),
                    pltpu.VMEM((2 * columns, 2 * hidden), BF),
                    pltpu.VMEM((len(steps), 2 * CAP, 2 * columns), BF),
                    pltpu.SemaphoreType.DMA((19,)),
                ],
                4 * 10**9,
                "gate_up",
            )(spot, *token_pieces, place, gain_columns, gate_up_weight, *up_takens)
            partial_hidden.update({k: list(flat[2 * i : 2 * i + 2]) for i, k in enumerate(steps)})

    with jax.named_scope("sum_hidden"):
        ahead_in = [to_z(partial_hidden[4][0], 1), None]
        back_in = [None, to_z(partial_hidden[4][1], -1)]
        for step in (3, 2, 1):
            for c in (1, 0):
                out = partial_hidden[step][c]
                if ahead_in[c] is not None:
                    out = plus(out, ahead_in[c])
                ahead_in[c] = to_z(out, 1)
                out = partial_hidden[NZ - step][1 - c]
                if back_in[1 - c] is not None:
                    out = plus(out, back_in[1 - c])
                back_in[1 - c] = to_z(out, -1)
        acts = []
        for c in range(2):
            full = partial_hidden[0][c].astype(F32) + ahead_in[c].astype(F32)
            full = full + back_in[c].astype(F32)
            factor = lax.rsqrt(full[:, 2 * hidden : 2 * hidden + 1] / model_width + NORM_EPS)
            full = full * factor
            acts.append((jax.nn.silu(full[:, :hidden]) * full[:, hidden : 2 * hidden]).astype(BF))

    with jax.named_scope("gather_hidden"):
        chunks = {0: acts}
        for step in (1, 2, 3):
            chunks[-step] = [to_z(chunks[1 - step][c], 1) for c in range(2)]
            chunks[step] = [to_z(chunks[step - 1][c], -1) for c in range(2)]
        chunks[4] = [to_z(chunks[-3][0], 1), to_z(chunks[3][1], -1)]

    with jax.named_scope("down"):
        groups = ((0, -1, 1, -2, 2), (-3, 3, 4))
        parts = []
        for steps in groups:
            count = len(steps)
            own_rows, other_rows = vmem_call(
                functools.partial(down_kernel, steps),
                (jax.ShapeDtypeStruct((2, count, columns, rows), BF),) * 2,
                [SMEM] + [VMEM] * (2 * count + 4),
                [
                    pltpu.VMEM((count * 128, hidden), BF),
                    pltpu.VMEM((2, columns, count * 128), BF),
                ],
                2 * 10**9,
                "down",
            )(
                spot,
                *[chunks[step][c] for step in steps for c in range(2)],
                down,
                down_taken,
                place,
                gain,
            )
            parts += [own_rows, swap_core(other_rows)]

    with jax.named_scope("return_rows"):
        gives = vmem_call(
            functools.partial(merge_kernel, groups),
            (jax.ShapeDtypeStruct((NY, columns, rows), BF),) * 4,
            [SMEM] + [VMEM] * 4,
            [],
            10**7,
            "merge",
        )(z.reshape(1), *parts)
        total = gives[0].astype(F32)
        for bits in (1, 2, 3):
            total = total + xor_x(gives[bits], bits).astype(F32)
        routed = total[0]
        for ahead in range(1, NY):
            routed = routed + from_y(total[ahead].astype(BF), -ahead).astype(F32)
        mine = lax.dynamic_slice_in_dim(mixed, xl * columns, columns, axis=0)
        return (mine.astype(F32) + routed).astype(BF).T


def solution(mesh):
    fine = Mesh(mesh.devices.reshape(2, NY, 2, 2, NZ), AXES)
    return jax.shard_map(
        body,
        mesh=fine,
        in_specs=(
            P(SEQ, EXP),
            P(SEQ, EXP),
            P(SEQ, EXP),
            P(SEQ, None),
            P(SEQ, None),
            P(EXP, None, None),
            P(EXP, None, None),
            P(EXP, None),
            P(EXP),
            P(SEQ, EXP, None),
            P(SEQ, None, EXP),
            P(SEQ, None),
            P(SEQ, None),
        ),
        out_specs=P(SEQ, EXP),
        check_vma=False,
    )
```
